256 devices in a mesh: member: 32 (over y, z), tile: 8 (over x, core).
Axes of the slice: x: 4, y: 4, z: 8, core: 2. Of those that a mesh axis runs over, the one named last changes fastest.
Arguments:
- realization_array: float32 [32, 4, 512, 512], P('member', None, 'tile'), may hold values from -6 to 6
- water_depth: float32 [512, 512], P('tile'), may hold values from 0.5 to 4
- wet_mask: int32 [512, 512], P('tile'), may hold values 0 or 1
- obs_cell: int32 [32768], P('tile'), may hold values from 0 to 32767, as said below
- obs_value: float32 [32768], P('tile'), may hold values from -8 to 8
- obs_error: float32 [32768], P('tile'), may hold values from 0.05 to 0.5
- celer_gain: float32 [32768], P('tile'), may hold values from 0.5 to 2
- obs_list: int32 [8, 128, 64], P('tile', 'member'), may hold values from 3584 to 8639, as said below
- obs_count: int32 [8, 128], P('tile', 'member'), may hold values from 32 to 64, as said below
Outputs:
- analysis: float32 [32, 4, 512, 512], P('member', None, 'tile')
The draws below stay inside these ranges and needn't reach their ends.
Inputs may be any that keep to these rules, and one draw needn't show every extreme that they name: `obs_cell`: observation o of a tile lies in cells o * S to o * S + S - 1 of that tile, S = 8. `obs_list`: the entries of one patch's list are distinct and name only observations of existing tiles. `obs_count`: some patch has a full list.
All inputs are finite; a program needn't handle non-finite values. No bound on the sum of `wet_mask` on one device may be relied on, other than what follows from the above.
Results may differ from the reference program's by a relative error of at most 0.0003.
Values sent between devices are 32-bit elements; how exact they have to be, the bound alone decides.
A program may use at most 128 MiB of HBM per device.

```python
import math
import jax
import jax.numpy as jnp
from jax import lax

PANEL_LINES = 64
MESH_SPAN_NORTH = 512
OBS_TILE = 4096
OBS_PATCH = 64
REGION_POINTS = 256
STEPS = 4
NS_ITERS = 14
MEMBERS = 32
SHEET_PANELS = 8
NX = 512
OBS = 32768
REGIONS_IN_PANEL = 128


def draw_obs_cell(key, part):
    key = jax.random.fold_in(key, 11)
    spacing = PANEL_LINES * MESH_SPAN_NORTH // OBS_TILE
    order = jnp.arange(OBS, dtype=jnp.int32) % OBS_TILE
    jitter = jax.random.randint(key, (OBS,), 0, spacing, dtype=jnp.int32)
    return order * spacing + jitter


def draw_obs_list(key, part):
    key = jax.random.fold_in(key, 23)
    radius = OBS_TILE // 8
    tile_iota = jnp.arange(SHEET_PANELS, dtype=jnp.int32)[:, None]
    patch_iota = jnp.arange(REGIONS_IN_PANEL, dtype=jnp.int32)[None, :]
    row_index = patch_iota * REGION_POINTS // MESH_SPAN_NORTH
    centre = OBS_TILE + row_index * OBS_TILE // PANEL_LINES
    lowest = jnp.where(tile_iota == 0, OBS_TILE, 0)
    highest = jnp.where(tile_iota == SHEET_PANELS - 1, 2 * OBS_TILE - 2 * radius, 3 * OBS_TILE - 2 * radius)
    start = jnp.clip(centre - radius, lowest, highest)
    position = jnp.arange(2 * radius, dtype=jnp.int32)
    scores = jax.random.randint(key, (SHEET_PANELS, REGIONS_IN_PANEL, 2 * radius), 0, 2 ** 16, dtype=jnp.int32)
    scores = scores * (2 * radius) + position
    ends = (position == 0) | (position == 2 * radius - 1)
    scores = scores + jnp.where(ends, 2 ** 28, 0).astype(jnp.int32)
    offsets = jax.lax.top_k(scores, OBS_PATCH)[1].astype(jnp.int32)
    return start[:, :, None] + offsets


def draw_obs_count(key, part):
    key = jax.random.fold_in(key, 37)
    first, second = jax.random.split(key)
    counts = jax.random.randint(first, (SHEET_PANELS * REGIONS_IN_PANEL,), OBS_PATCH // 2, OBS_PATCH + 1, dtype=jnp.int32)
    chosen = jax.random.randint(second, (), 0, SHEET_PANELS * REGIONS_IN_PANEL, dtype=jnp.int32)
    counts = jnp.where(jnp.arange(SHEET_PANELS * REGIONS_IN_PANEL, dtype=jnp.int32) == chosen, OBS_PATCH, counts)
    return counts.reshape(SHEET_PANELS, REGIONS_IN_PANEL)


def place_ends(values, own_key, least, largest):
    longest = values.shape.index(max(values.shape))
    spots = []
    for shift in (0, 1):
        where = [jax.random.randint(jax.random.fold_in(own_key, axis), (), 0, length) for axis, length in enumerate(values.shape)]
        where[longest] = (where[longest] + shift) % values.shape[longest]
        spots.append(tuple(where))
    return values.at[spots[0]].set(least).at[spots[1]].set(largest)


def levels(rng, shape, cuts, least, top_value):
    loudness, own = 1.0, jax.random.fold_in(rng, 6)
    for axis_at, shards_of in cuts:
        draws = jnp.exp(jax.random.uniform(jax.random.fold_in(own, axis_at), (shards_of,), jnp.float32, least / len(cuts), top_value / len(cuts)))
        loudness = loudness * jnp.repeat(draws, shape[axis_at] // shards_of).reshape([-1 if axis == axis_at else 1 for axis in range(len(shape))])
    return loudness


def bell_draw(rng, extent, scale, bound, pieces=(), kind=jnp.bfloat16):
    entries = scale * jax.random.normal(rng, extent, jnp.float32)
    if pieces:
        entries = entries * levels(rng, extent, pieces, -0.22, 0.18)
    return jnp.clip(entries, -bound, bound).astype(kind)


def setup_inputs(seed: int = 0) -> dict:
    arg_keys = jax.random.split(jax.random.key(seed), 10)
    realization_array = bell_draw(arg_keys[0], (MEMBERS, 4, NX, MESH_SPAN_NORTH), 1.0, 6.0, ((0, 32), (2, 8)), jnp.float32)
    water_depth = jnp.clip(jnp.exp(math.log(4.0) - 2.0794415 * jax.random.uniform(arg_keys[1], (NX, MESH_SPAN_NORTH), jnp.float32) ** levels(arg_keys[1], (NX, MESH_SPAN_NORTH), ((0, 8),), -0.2, 0.2)), 0.5, 4.0)
    wet_mask = place_ends((jax.random.randint(arg_keys[2], (NX, MESH_SPAN_NORTH), 0, 8) < 7).astype(jnp.int32), jax.random.fold_in(arg_keys[2], 1), 0, 1)
    obs_cell = draw_obs_cell(jax.random.fold_in(arg_keys[9], 71), 0)
    obs_value = bell_draw(arg_keys[4], (OBS,), 1.5, 8.0, ((0, 8),), jnp.float32)
    obs_error = jnp.clip(jnp.exp(math.log(0.5) - 2.3025851 * jax.random.uniform(arg_keys[5], (OBS,), jnp.float32) ** levels(arg_keys[5], (OBS,), ((0, 8),), -0.2, 0.2)), 0.05, 0.5)
    celer_gain = jnp.clip(jnp.exp(math.log(2.0) - 1.3862944 * jax.random.uniform(arg_keys[6], (OBS,), jnp.float32) ** levels(arg_keys[6], (OBS,), ((0, 8),), -0.2, 0.2)), 0.5, 2.0)
    obs_list = draw_obs_list(jax.random.fold_in(arg_keys[9], 71), 0)
    obs_count = draw_obs_count(jax.random.fold_in(arg_keys[9], 71), 0)
    return dict(realization_array=realization_array, water_depth=water_depth, wet_mask=wet_mask, obs_cell=obs_cell, obs_value=obs_value, obs_error=obs_error, celer_gain=celer_gain, obs_list=obs_list, obs_count=obs_count)


FRICTION = 0.98
PRESSURE = 0.25
DIVERGE = 0.25
FORCING = 0.05
UPWIND = 0.4
DAMPING = 0.02
HIGH = lax.Precision.HIGHEST

def along_y(field):
    padded = jnp.pad(field, ((0, 0), (1, 1)))
    return (padded[:, 2:], padded[:, :-2])

def advance(water_elevation, eastward_velocity, northward_velocity, swell_intensity, water_depth, wet_float):
    level_pad = jnp.pad(water_elevation, ((1, 1), (0, 0)))
    new_x = wet_float * (FRICTION * eastward_velocity - PRESSURE * (level_pad[2:] - level_pad[:-2]))
    level_up, level_down = along_y(water_elevation)
    new_y = wet_float * (FRICTION * northward_velocity - PRESSURE * (level_up - level_down))
    flux_x = jnp.pad(water_depth * new_x, ((1, 1), (0, 0)))
    flux_up, flux_down = along_y(water_depth * new_y)
    new_surface = wet_float * (water_elevation - DIVERGE * (flux_x[2:] - flux_x[:-2] + flux_up - flux_down) + FORCING * swell_intensity)
    energy_pad = jnp.pad(swell_intensity, ((1, 0), (0, 0)))
    new_energy = wet_float * (swell_intensity - UPWIND * (swell_intensity - energy_pad[:-1]) - DAMPING * swell_intensity)
    return (new_surface, new_x, new_y, new_energy)

def mat_mul(left, right):
    return jnp.matmul(left, right, precision=HIGH)

def mix_weights(gram, proj):
    count = gram.shape[-1]
    eye = jnp.eye(count, dtype=jnp.float32)
    amat = gram + (count - 1.0) * eye
    trace_sum = jnp.trace(amat, axis1=1, axis2=2)
    current = amat / trace_sum[:, None, None]
    inverse = jnp.broadcast_to(eye, amat.shape)
    for sweep in range(NS_ITERS):
        factor = 1.5 * eye - 0.5 * mat_mul(inverse, current)
        current = mat_mul(current, factor)
        inverse = mat_mul(factor, inverse)
    root = inverse / jnp.sqrt(trace_sum)[:, None, None]
    covar = mat_mul(root, root)
    wbar = jnp.einsum('pkl,pl->pk', covar, proj, precision=HIGH)
    wtot = jnp.sqrt(count - 1.0) * root + wbar[:, :, None]
    return wtot - lax.optimization_barrier(jnp.mean(wtot, axis=1, keepdims=True)) + 1.0 / count

def reference(realization_array, water_depth, wet_mask, obs_cell, obs_value, obs_error, celer_gain, obs_list, obs_count):
    wet_float = wet_mask.astype(jnp.float32)

    def integrate_realization(state):
        water_elevation, eastward_velocity, northward_velocity, swell_intensity = (state[0], state[1], state[2], state[3])
        for sweep in range(STEPS):
            water_elevation, eastward_velocity, northward_velocity, swell_intensity = advance(water_elevation, eastward_velocity, northward_velocity, swell_intensity, water_depth, wet_float)
        return jnp.stack([water_elevation, eastward_velocity, northward_velocity, swell_intensity])
    predicted_fields = lax.map(integrate_realization, realization_array)
    realization_pile = predicted_fields.shape[0]
    elevation_panels = predicted_fields[:, 0].reshape(realization_pile, SHEET_PANELS, PANEL_LINES * MESH_SPAN_NORTH)
    cells = obs_cell.reshape(SHEET_PANELS, OBS_TILE)
    equivalents = jnp.take_along_axis(elevation_panels, cells[None], axis=2) * celer_gain.reshape(SHEET_PANELS, OBS_TILE)[None]
    equivalents = equivalents.reshape(realization_pile, OBS)
    tile_iota = jnp.arange(SHEET_PANELS, dtype=jnp.int32)[:, None, None]
    global_idx = (tile_iota * OBS_TILE - OBS_TILE + obs_list).astype(jnp.int32)
    picked = equivalents[:, global_idx]
    value = obs_value[global_idx]
    error = obs_error[global_idx]
    patch_iota = jnp.arange(REGIONS_IN_PANEL, dtype=jnp.int32)
    row_index = patch_iota * REGION_POINTS // MESH_SPAN_NORTH
    centre = OBS_TILE + row_index * OBS_TILE // PANEL_LINES
    radius = OBS_TILE // 8
    dist = (obs_list - centre[None, :, None]).astype(jnp.float32) / radius
    live = jnp.arange(OBS_PATCH, dtype=jnp.int32)[None, None, :] < obs_count[:, :, None]
    precision = jnp.where(live, 1.0 / ((1.0 + 4.0 * dist * dist) * error), 0.0)
    mean_eq = lax.optimization_barrier(jnp.mean(picked, axis=0))
    spread = picked - mean_eq[None]
    gram = jnp.einsum('ktpo,ltpo->tpkl', spread * precision[None], spread, precision=HIGH)
    proj = jnp.einsum('ktpo,tpo->tpk', spread, precision * (value - mean_eq), precision=HIGH)
    mix = mix_weights(gram.reshape(SHEET_PANELS * REGIONS_IN_PANEL, realization_pile, realization_pile), proj.reshape(SHEET_PANELS * REGIONS_IN_PANEL, realization_pile))
    mix = mix.reshape(SHEET_PANELS, REGIONS_IN_PANEL, realization_pile, realization_pile)
    panel_sequence = predicted_fields.reshape(realization_pile, 4, SHEET_PANELS, REGIONS_IN_PANEL, REGION_POINTS)
    analysis = jnp.einsum('kftpc,tpkm->mftpc', panel_sequence, mix, precision=HIGH)
    return analysis.reshape(realization_pile, 4, NX, MESH_SPAN_NORTH)
```

```python
import functools

import jax
import jax.numpy as jnp
from jax import lax
from jax.experimental import pallas as pl
from jax.experimental.pallas import tpu as pltpu
from jax.sharding import PartitionSpec as P

MESH = pl.DeviceIdType.MESH
HIGH = lax.Precision.HIGHEST
F32 = jnp.float32
BF16 = jnp.bfloat16

REGION_POINTS = 256
STEPS = 4
NS_ITERS = 14
SPACING = 8

FRICTION = 0.98
PRESSURE = 0.25
DIVERGE = 0.25
FORCING = 0.05
UPWIND = 0.4
DAMPING = 0.02

LANES = 128
GUARD = 8
HALO = 16
OBS_HALO = 8
TABLE_PAD = 8


def iota(shape, dim):
    return lax.broadcasted_iota(jnp.int32, shape, dim)


def dot(left, right, precision=None):
    return lax.dot_general(
        left, right, (((1,), (0,)), ((), ())), precision=precision, preferred_element_type=F32
    )


def split(x):
    high = x.astype(BF16)
    return high, (x - high.astype(F32)).astype(BF16)


def dot3(left, right):
    left_high, left_low = split(left)
    right_high, right_low = split(right)
    return (dot(left_low, right_high) + dot(left_high, right_low)) + dot(left_high, right_high)


def lookup(table, first, last, high, low):
    found = jnp.zeros(high.shape, table.dtype)
    for row in range(first, last):
        line = jnp.broadcast_to(table[row : row + 1, :], high.shape)
        found = jnp.where(
            high == row,
            jnp.take_along_axis(line, low, axis=1, mode="promise_in_bounds"),
            found,
        )
    return found


def kernel(
    members,
    tiles,
    grid_rows,
    state_ref,
    depth_ref,
    wet_ref,
    cell_ref,
    gain_ref,
    value_ref,
    error_ref,
    list_ref,
    count_ref,
    out_ref,
    state_ext,
    depth_ext,
    wet_ext,
    cell_ext,
    gain_ext,
    value_ext,
    error_ext,
    work,
    hwork,
    wwork,
    flux,
    cross,
    pack,
    lists,
    table,
    pick_out,
    pick_in,
    slab_out,
    slab_in,
    mix_out,
    back_in,
    rows_out,
    local_sem,
    halo_send,
    halo_recv,
    group_send,
    group_recv,
):
    me = lax.axis_index("member")
    tile = lax.axis_index("tile")
    above = lax.rem(tile + tiles - 1, tiles)
    below = lax.rem(tile + 1, tiles)
    ext_rows = grid_rows + 2 * HALO
    lane_tiles = 4
    obs_tile = grid_rows * 64
    radius = obs_tile // 8
    own_table = obs_tile // LANES
    table_rows = own_table + 2 * TABLE_PAD
    others = members - 1

    own_rows = pl.ds(HALO, grid_rows)
    own_lines = pl.ds(TABLE_PAD, own_table)
    tables = (
        (cell_ref, cell_ext),
        (gain_ref, gain_ext),
        (value_ref, value_ext),
        (error_ref, error_ext),
    )
    local = [
        pltpu.make_async_copy(state_ref.at[0], state_ext.at[:, own_rows], local_sem.at[0]),
        pltpu.make_async_copy(depth_ref, depth_ext.at[own_rows], local_sem.at[1]),
        pltpu.make_async_copy(wet_ref, wet_ext.at[own_rows], local_sem.at[2]),
    ] + [
        pltpu.make_async_copy(ref, ext.at[own_lines], local_sem.at[3 + i])
        for i, (ref, ext) in enumerate(tables)
    ]
    for copy in local:
        copy.start()

    pack[...] = jnp.zeros(pack.shape, jnp.int32)
    pack[0:4, 0:64] = list_ref[0]
    packed = pack[...]
    turned = pltpu.roll(packed, 64, axis=1)
    left_half = iota((1, LANES), 1) < 64
    own_list = jnp.concatenate(
        [
            jnp.where(left_half, packed[0:1], turned[1:2]),
            jnp.where(left_half, packed[2:3], turned[3:4]),
        ],
        axis=0,
    )
    lists[me] = own_list

    barrier = pltpu.get_barrier_semaphore()

    def greet(step, carry):
        peer = lax.rem(me + step, members)
        pl.semaphore_signal(barrier, inc=1, device_id={"member": peer}, device_id_type=MESH)
        return carry

    pl.semaphore_signal(barrier, inc=1, device_id={"tile": above}, device_id_type=MESH)
    pl.semaphore_signal(barrier, inc=1, device_id={"tile": below}, device_id_type=MESH)
    lax.fori_loop(1, members, greet, 0)
    pl.semaphore_wait(barrier, others + 2)

    halos = []
    for way, (target, source_row, target_row, source_line, target_line) in enumerate(
        (
            (below, grid_rows - HALO, 0, own_table - TABLE_PAD, 0),
            (above, 0, HALO + grid_rows, 0, TABLE_PAD + own_table),
        )
    ):
        source_rows, target_rows = pl.ds(source_row, HALO), pl.ds(target_row, HALO)
        source_lines, target_lines = pl.ds(source_line, TABLE_PAD), pl.ds(target_line, TABLE_PAD)
        pairs = [
            (state_ref.at[0, :, source_rows], state_ext.at[:, target_rows]),
            (depth_ref.at[source_rows], depth_ext.at[target_rows]),
            (wet_ref.at[source_rows], wet_ext.at[target_rows]),
        ] + [(ref.at[source_lines], ext.at[target_lines]) for ref, ext in tables]
        for i, (source, destination) in enumerate(pairs):
            copy = pltpu.make_async_remote_copy(
                src_ref=source,
                dst_ref=destination,
                send_sem=halo_send.at[way, i],
                recv_sem=halo_recv.at[way, i],
                device_id={"tile": target},
                device_id_type=MESH,
            )
            copy.start()
            halos.append(copy)

    def to_group(which, source, destination):
        def send(step, carry):
            peer = lax.rem(me + step, members)
            pltpu.make_async_remote_copy(
                src_ref=source(peer),
                dst_ref=destination,
                send_sem=group_send.at[which],
                recv_sem=group_recv.at[which],
                device_id={"member": peer},
                device_id_type=MESH,
            ).start()
            return carry

        lax.fori_loop(1, members, send, 0)

    def group_done(sems, which, ref, size):
        part = ref.at[pl.ds(0, size)]
        pltpu.make_async_copy(part, part, sems.at[which]).wait()

    to_group(0, lambda peer: lists.at[me], lists.at[me])

    blank = jnp.zeros((lane_tiles, GUARD, LANES), F32)
    for field in range(4):
        work[field, :, 0:GUARD, :] = blank
        work[field, :, GUARD + ext_rows :, :] = blank
    flux[:, 0:GUARD, :] = blank
    flux[:, GUARD + ext_rows :, :] = blank

    for copy in local:
        copy.wait()
    for copy in halos:
        copy.wait_recv()

    for start in range(0, ext_rows, 8):
        rows = slice(start, start + 8)
        put = slice(GUARD + start, GUARD + start + 8)
        if start < HALO:
            inside = tile > 0
        elif start >= HALO + grid_rows:
            inside = tile < tiles - 1
        else:
            inside = None
        for at in range(lane_tiles):
            lanes = slice(at * LANES, (at + 1) * LANES)
            parts = [state_ext[field, rows, lanes] for field in range(4)]
            parts.append(wet_ext[rows, lanes].astype(F32))
            if inside is not None:
                parts = [jnp.where(inside, part, 0.0) for part in parts]
            for field in range(4):
                work[field, at, put, :] = parts[field]
            wwork[at, put, :] = parts[4]
            hwork[at, put, :] = depth_ext[rows, lanes]

    first_lane = iota((8, LANES), 1) == 0
    last_lane = iota((8, LANES), 1) == LANES - 1

    def across(parts):
        nothing = jnp.zeros((8, LANES), F32)
        up = [pltpu.roll(part, LANES - 1, axis=1) for part in parts] + [nothing]
        down = [nothing] + [pltpu.roll(part, 1, axis=1) for part in parts]
        return [
            jnp.where(last_lane, up[at + 1], up[at])
            - jnp.where(first_lane, down[at], down[at + 1])
            for at in range(lane_tiles)
        ]

    def advance(step, carry):
        for start in range(GUARD, GUARD + ext_rows, 8):
            rows = slice(start, start + 8)
            after = slice(start + 1, start + 9)
            before = slice(start - 1, start + 7)
            slope_y = across([work[0, at, rows, :] for at in range(lane_tiles)])
            flow = []
            for at in range(lane_tiles):
                wet = wwork[at, rows, :]
                height = hwork[at, rows, :]
                slope_x = work[0, at, after, :] - work[0, at, before, :]
                new_x = wet * (FRICTION * work[1, at, rows, :] - PRESSURE * slope_x)
                new_y = wet * (FRICTION * work[2, at, rows, :] - PRESSURE * slope_y[at])
                work[1, at, rows, :] = new_x
                work[2, at, rows, :] = new_y
                flux[at, rows, :] = height * new_x
                flow.append(height * new_y)
            for at, part in enumerate(across(flow)):
                cross[at, rows, :] = part
        for start in range(GUARD + ext_rows - 8, 0, -8):
            rows = slice(start, start + 8)
            after = slice(start + 1, start + 9)
            before = slice(start - 1, start + 7)
            for at in range(lane_tiles):
                wet = wwork[at, rows, :]
                level = work[0, at, rows, :]
                energy = work[3, at, rows, :]
                spill = (flux[at, after, :] - flux[at, before, :]) + cross[at, rows, :]
                work[0, at, rows, :] = wet * (level - DIVERGE * spill + FORCING * energy)
                work[3, at, rows, :] = wet * (
                    energy - UPWIND * (energy - work[3, at, before, :]) - DAMPING * energy
                )
        return carry

    lax.fori_loop(0, STEPS, advance, 0)

    first_line = TABLE_PAD - OBS_HALO // 2
    last_line = TABLE_PAD + own_table + OBS_HALO // 2
    offset = (cell_ext[...] & (SPACING - 1)).astype(BF16)
    place = iota((1, LANES), 1) & (SPACING - 1)
    equiv = jnp.zeros((table_rows, LANES), F32)
    for parity in range(2):
        for at in range(lane_tiles):
            owner = iota((LANES, LANES), 0) // SPACING + (parity * 64 + at * 16)
            gather = (owner == iota((LANES, LANES), 1)).astype(BF16)
            owner_t = iota((LANES, LANES), 1) // SPACING + (parity * 64 + at * 16)
            scatter = (owner_t == iota((LANES, LANES), 0)).astype(BF16)
            wanted = dot(offset, scatter).astype(jnp.int32) == place
            level = work[0, at, pl.ds(GUARD + parity, table_rows, stride=2), :]
            level = jnp.where(wanted, level, 0.0)
            high, rest = split(level)
            middle, low = split(level - high.astype(F32))
            equiv = equiv + ((dot(low, gather) + dot(middle, gather)) + dot(high, gather))
    table[...] = equiv * gain_ext[...]

    group_done(group_recv, 0, lists, others)
    base = obs_tile - TABLE_PAD * LANES
    for start in range(0, members, 4):
        slots = jnp.concatenate([lists[start + i] for i in range(4)], axis=0) - base
        found = lookup(
            table, first_line, last_line, slots // LANES, slots & (LANES - 1)
        )
        for i in range(4):
            pick_out[start + i] = found[2 * i : 2 * i + 2, :]
    pick_in[me] = pick_out[me]
    to_group(1, lambda peer: pick_out.at[peer], pick_in.at[me])

    slab = 8 * lane_tiles
    for field in range(4):
        for at in range(lane_tiles):
            for row in range(2):
                slab_out[pl.ds(at * 8 + field * 2 + row, members, stride=slab), :] = work[
                    field, at, pl.ds(GUARD + HALO + row, members, stride=2), :
                ]
    own_slab = pl.ds(pl.multiple_of(me * slab, slab), slab)
    slab_in[own_slab, :] = slab_out[own_slab, :]
    to_group(
        2,
        lambda peer: slab_out.at[pl.ds(pl.multiple_of(peer * slab, slab), slab)],
        slab_in.at[own_slab],
    )

    names = jnp.concatenate([own_list] * 4, axis=0)
    slots = names - base
    high, low = slots // LANES, slots & (LANES - 1)
    value = lookup(value_ext, first_line, last_line, high, low)
    error = lookup(error_ext, first_line, last_line, high, low)
    value, error = value[0:2], error[0:2]
    row_index = me * 2 + iota((2, LANES), 0)
    centre = obs_tile + row_index * 64
    dist = (own_list - centre).astype(F32) / radius
    counts = count_ref[...]
    slot = iota((1, LANES), 1) & 63
    limit = jnp.concatenate(
        [
            jnp.where(
                left_half, counts[0:1, 2 * i : 2 * i + 1], counts[0:1, 2 * i + 1 : 2 * i + 2]
            )
            for i in range(2)
        ],
        axis=0,
    )
    live = slot < limit
    precision = jnp.where(live, 1.0 / ((1.0 + 4.0 * dist * dist) * error), 0.0)

    group_done(group_recv, 1, pick_in, others)
    size = 4 * members
    weighted, spreads, innovations = [], [], []
    for i in range(2):
        picked = pick_in[:, i, :]
        mean_eq = jnp.sum(picked, axis=0, keepdims=True) * (1.0 / members)
        spread = picked - mean_eq
        weighted.append(spread * precision[i : i + 1])
        spreads.append(spread)
        innovations.append(value[i : i + 1] - mean_eq)
    block_row = iota((size, LANES), 0) // members
    halves = (iota((size, LANES), 1) // 64 == block_row % 2, block_row // 2)

    def blocks(parts):
        return jnp.concatenate(
            [
                jnp.where(
                    jnp.logical_and(halves[0], halves[1] == i),
                    jnp.concatenate([parts[i]] * 4, axis=0),
                    0.0,
                )
                for i in range(2)
            ],
            axis=1,
        )

    weighted = blocks(weighted)
    spread = blocks(spreads)
    gram = lax.dot_general(
        weighted, spread, (((1,), (1,)), ((), ())), precision=HIGH, preferred_element_type=F32
    )
    proj = jnp.sum(weighted * jnp.concatenate(innovations, axis=1), axis=1, keepdims=True)

    line, column = iota((size, size), 0), iota((size, size), 1)
    diagonal = line == column
    same = line // members == column // members
    eye = jnp.where(diagonal, 1.0, 0.0)
    amat = gram + (members - 1.0) * eye
    trace = jnp.sum(jnp.where(diagonal, amat, 0.0), axis=1, keepdims=True)
    trace = jnp.concatenate(
        [
            jnp.broadcast_to(
                jnp.sum(trace[i * members : (i + 1) * members], axis=0, keepdims=True),
                (members, 1),
            )
            for i in range(4)
        ],
        axis=0,
    )

    def sweep(step, carry):
        current, inverse = carry
        factor = 1.5 * eye - 0.5 * dot3(inverse, current)
        return dot3(current, factor), dot3(factor, inverse)

    current, inverse = lax.fori_loop(0, NS_ITERS, sweep, (amat / trace, eye))
    root = inverse / jnp.sqrt(trace)
    wbar = dot3(root, dot3(root, jnp.broadcast_to(proj, (size, size))))
    wtot = jnp.where(same, (members - 1.0) ** 0.5 * root + wbar, 0.0)
    mean = jnp.sum(wtot, axis=0, keepdims=True) * (1.0 / members)
    mix = jnp.where(same, wtot - mean + 1.0 / members, 0.0)
    mix = jnp.transpose(mix)

    group_done(group_recv, 2, slab_in, others * slab)
    for field in range(4):
        for half in range(2):
            inputs = jnp.concatenate(
                [
                    jnp.concatenate(
                        [
                            slab_in[
                                pl.ds((side * 2 + half) * 8 + field * 2 + row, members, stride=slab), :
                            ]
                            for side in range(2)
                        ],
                        axis=0,
                    )
                    for row in range(2)
                ],
                axis=0,
            )
            mixed = dot3(mix, inputs)
            for row in range(2):
                for side in range(2):
                    patch = row * 2 + side
                    mix_out[
                        pl.ds((side * 2 + half) * 8 + field * 2 + row, members, stride=slab), :
                    ] = mixed[patch * members : (patch + 1) * members]
    back_in[own_slab, :] = mix_out[own_slab, :]
    to_group(
        3,
        lambda peer: mix_out.at[pl.ds(pl.multiple_of(peer * slab, slab), slab)],
        back_in.at[own_slab],
    )
    group_done(group_recv, 3, back_in, others * slab)
    for field in range(4):
        for at in range(lane_tiles):
            for row in range(2):
                rows_out[field, at, pl.ds(row, members, stride=2), :] = back_in[
                    pl.ds(at * 8 + field * 2 + row, members, stride=slab), :
                ]
    for field in range(4):
        for at in range(lane_tiles):
            out_ref[0, field, :, at * LANES : (at + 1) * LANES] = rows_out[field, at]

    for copy in halos:
        copy.wait_send()
    group_done(group_send, 0, lists, others)
    group_done(group_send, 1, pick_out, others)
    group_done(group_send, 2, slab_out, others * slab)
    group_done(group_send, 3, mix_out, others * slab)


def body(
    realization_array,
    water_depth,
    wet_mask,
    obs_cell,
    obs_value,
    obs_error,
    celer_gain,
    obs_list,
    obs_count,
):
    members = lax.axis_size("member")
    tiles = lax.axis_size("tile")
    grid_rows, width = water_depth.shape
    ext_rows = grid_rows + 2 * HALO
    lane_tiles = width // LANES
    own_table = obs_cell.shape[0] // LANES
    table_rows = own_table + 2 * TABLE_PAD
    slab_rows = members * 8 * lane_tiles
    deep = ext_rows + 2 * GUARD
    as_lines = lambda array: array.reshape(own_table, LANES)
    far = pl.BlockSpec(memory_space=pl.ANY)
    near = pl.BlockSpec(memory_space=pltpu.VMEM)
    return pl.pallas_call(
        functools.partial(kernel, members, tiles, grid_rows),
        out_shape=jax.ShapeDtypeStruct(realization_array.shape, F32),
        in_specs=[far] * 7 + [near] * 2,
        out_specs=near,
        scratch_shapes=[
            pltpu.VMEM((4, ext_rows, width), F32),
            pltpu.VMEM((ext_rows, width), F32),
            pltpu.VMEM((ext_rows, width), jnp.int32),
            pltpu.VMEM((table_rows, LANES), jnp.int32),
            pltpu.VMEM((table_rows, LANES), F32),
            pltpu.VMEM((table_rows, LANES), F32),
            pltpu.VMEM((table_rows, LANES), F32),
            pltpu.VMEM((4, lane_tiles, deep, LANES), F32),
            pltpu.VMEM((lane_tiles, deep, LANES), F32),
            pltpu.VMEM((lane_tiles, deep, LANES), F32),
            pltpu.VMEM((lane_tiles, deep, LANES), F32),
            pltpu.VMEM((lane_tiles, deep, LANES), F32),
            pltpu.VMEM((8, LANES), jnp.int32),
            pltpu.VMEM((members, 2, LANES), jnp.int32),
            pltpu.VMEM((table_rows, LANES), F32),
            pltpu.VMEM((members, 2, LANES), F32),
            pltpu.VMEM((members, 2, LANES), F32),
            pltpu.VMEM((slab_rows, LANES), F32),
            pltpu.VMEM((slab_rows, LANES), F32),
            pltpu.VMEM((slab_rows, LANES), F32),
            pltpu.VMEM((slab_rows, LANES), F32),
            pltpu.VMEM((4, lane_tiles, grid_rows, LANES), F32),
            pltpu.SemaphoreType.DMA((7,)),
            pltpu.SemaphoreType.DMA((2, 7)),
            pltpu.SemaphoreType.DMA((2, 7)),
            pltpu.SemaphoreType.DMA((4,)),
            pltpu.SemaphoreType.DMA((4,)),
        ],
        compiler_params=pltpu.CompilerParams(
            collective_id=0, has_side_effects=True, vmem_limit_bytes=32 * 1024 * 1024
        ),
    )(
        realization_array,
        water_depth,
        wet_mask,
        as_lines(obs_cell),
        as_lines(celer_gain),
        as_lines(obs_value),
        as_lines(obs_error),
        obs_list,
        obs_count,
    )


def solution(mesh):
    return jax.shard_map(
        body,
        mesh=mesh,
        in_specs=(
            P("member", None, "tile", None),
            P("tile", None),
            P("tile", None),
            P("tile"),
            P("tile"),
            P("tile"),
            P("tile"),
            P("tile", "member", None),
            P("tile", "member"),
        ),
        out_specs=P("member", None, "tile", None),
        check_vma=False,
    )
```

```python
import functools

import jax
import jax.numpy as jnp
from jax import lax
from jax.experimental import pallas as pl
from jax.experimental.pallas import tpu as pltpu
from jax.sharding import PartitionSpec as P

MESH = pl.DeviceIdType.MESH
HIGH = lax.Precision.HIGHEST
F32 = jnp.float32
BF16 = jnp.bfloat16

REGION_POINTS = 256
STEPS = 4
NS_ITERS = 14
SPACING = 8

FRICTION = 0.98
PRESSURE = 0.25
DIVERGE = 0.25
FORCING = 0.05
UPWIND = 0.4
DAMPING = 0.02

LANES = 128
GUARD = 8
HALO = 16
OBS_HALO = 8
TABLE_PAD = 8


def iota(shape, dim):
    return lax.broadcasted_iota(jnp.int32, shape, dim)


def dot(left, right, precision=None):
    return lax.dot_general(
        left, right, (((1,), (0,)), ((), ())), precision=precision, preferred_element_type=F32
    )


def split(x):
    high = x.astype(BF16)
    return high, (x - high.astype(F32)).astype(BF16)


def dot3(left, right):
    left_high, left_low = split(left)
    right_high, right_low = split(right)
    rows = left.shape[0]
    both = dot(jnp.concatenate([left_high, left_low], axis=0), right_high)
    return (both[rows:] + dot(left_high, right_low)) + both[:rows]


def exact_dot(left, ones):
    high, _ = split(left)
    middle, low = split(left - high.astype(F32))
    rows = left.shape[0]
    parts = dot(jnp.concatenate([high, middle, low], axis=0), ones)
    return (parts[2 * rows :] + parts[rows : 2 * rows]) + parts[:rows]


def lookup(table, first, last, high, low):
    found = jnp.zeros(high.shape, table.dtype)
    for row in range(first, last):
        line = jnp.broadcast_to(table[row : row + 1, :], high.shape)
        found = jnp.where(
            high == row,
            jnp.take_along_axis(line, low, axis=1, mode="promise_in_bounds"),
            found,
        )
    return found


def kernel(
    members,
    tiles,
    grid_rows,
    state_ref,
    depth_ref,
    wet_ref,
    cell_ref,
    gain_ref,
    value_ref,
    error_ref,
    list_ref,
    count_ref,
    out_ref,
    state_ext,
    depth_ext,
    wet_ext,
    cell_ext,
    gain_ext,
    value_ext,
    error_ext,
    work,
    edge,
    hwork,
    wwork,
    flux,
    cross,
    edge_flux,
    edge_cross,
    raw_list,
    raw_count,
    pack,
    lists,
    table,
    pick_out,
    pick_in,
    slab_out,
    slab_in,
    mix_out,
    back_in,
    rows_out,
    local_sem,
    halo_send,
    halo_recv,
    group_send,
    group_recv,
):
    me = lax.axis_index("member")
    tile = lax.axis_index("tile")
    above = lax.rem(tile + tiles - 1, tiles)
    below = lax.rem(tile + 1, tiles)
    ext_rows = grid_rows + 2 * HALO
    lane_tiles = 4
    obs_tile = grid_rows * 64
    radius = obs_tile // 8
    own_table = obs_tile // LANES
    table_rows = own_table + 2 * TABLE_PAD
    others = members - 1

    barrier = pltpu.get_barrier_semaphore()

    def greet(step, carry):
        peer = lax.rem(me + step, members)
        pl.semaphore_signal(barrier, inc=1, device_id={"member": peer}, device_id_type=MESH)
        return carry

    pl.semaphore_signal(barrier, inc=1, device_id={"tile": above}, device_id_type=MESH)
    pl.semaphore_signal(barrier, inc=1, device_id={"tile": below}, device_id_type=MESH)
    lax.fori_loop(1, members, greet, 0)

    own_rows = pl.ds(HALO, grid_rows)
    own_lines = pl.ds(TABLE_PAD, own_table)
    tables = (
        (cell_ref, cell_ext),
        (gain_ref, gain_ext),
        (value_ref, value_ext),
        (error_ref, error_ext),
    )
    pairs = [
        (list_ref.at[0], raw_list),
        (count_ref, raw_count),
        (state_ref.at[0], state_ext.at[:, own_rows]),
        (depth_ref, depth_ext.at[own_rows]),
        (wet_ref, wet_ext.at[own_rows]),
    ] + [(ref, ext.at[own_lines]) for ref, ext in tables]
    local = [
        pltpu.make_async_copy(source, destination, local_sem.at[i])
        for i, (source, destination) in enumerate(pairs)
    ]
    for copy in local:
        copy.start()

    nothing = jnp.zeros((8, LANES), F32)
    strip = 2 * HALO
    own_start = GUARD + HALO
    own_end = own_start + grid_rows
    for at in range(lane_tiles):
        for field in (0, 3):
            work[field, at, own_start - 8 : own_start, :] = nothing
            work[field, at, own_end : own_end + 8, :] = nothing
            for side in range(2):
                edge[side, field, at, 0:GUARD, :] = nothing
                edge[side, field, at, GUARD + strip :, :] = nothing
        flux[at, own_start - 8 : own_start, :] = nothing
        flux[at, own_end : own_end + 8, :] = nothing
        for side in range(2):
            edge_flux[side, at, 0:GUARD, :] = nothing
            edge_flux[side, at, GUARD + strip :, :] = nothing
    pack[...] = jnp.zeros(pack.shape, jnp.int32)

    pl.semaphore_wait(barrier, others + 2)

    halos = []
    for way, (target, source_row, target_row, source_line, target_line) in enumerate(
        (
            (below, grid_rows - HALO, 0, own_table - TABLE_PAD, 0),
            (above, 0, HALO + grid_rows, 0, TABLE_PAD + own_table),
        )
    ):
        source_rows, target_rows = pl.ds(source_row, HALO), pl.ds(target_row, HALO)
        source_lines, target_lines = pl.ds(source_line, TABLE_PAD), pl.ds(target_line, TABLE_PAD)
        pairs = [
            (state_ref.at[0, :, source_rows], state_ext.at[:, target_rows]),
            (depth_ref.at[source_rows], depth_ext.at[target_rows]),
            (wet_ref.at[source_rows], wet_ext.at[target_rows]),
        ] + [(ref.at[source_lines], ext.at[target_lines]) for ref, ext in tables]
        for i, (source, destination) in enumerate(pairs):
            copy = pltpu.make_async_remote_copy(
                src_ref=source,
                dst_ref=destination,
                send_sem=halo_send.at[way, i],
                recv_sem=halo_recv.at[way, i],
                device_id={"tile": target},
                device_id_type=MESH,
            )
            copy.start()
            halos.append(copy)

    def send(which, peer, source, destination):
        pltpu.make_async_remote_copy(
            src_ref=source,
            dst_ref=destination,
            send_sem=group_send.at[which],
            recv_sem=group_recv.at[which],
            device_id={"member": peer},
            device_id_type=MESH,
        ).start()

    def to_group(which, source, destination):
        def one(step, carry):
            peer = lax.rem(me + step, members)
            send(which, peer, source(peer), destination)
            return carry

        lax.fori_loop(1, members, one, 0)

    def group_done(sems, which, ref, size):
        part = ref.at[pl.ds(0, size)]
        pltpu.make_async_copy(part, part, sems.at[which]).wait()

    local[0].wait()
    pack[0:4, 0:64] = raw_list[...]
    packed = pack[...]
    turned = pltpu.roll(packed, 64, axis=1)
    left_half = iota((1, LANES), 1) < 64
    own_list = jnp.concatenate(
        [
            jnp.where(left_half, packed[0:1], turned[1:2]),
            jnp.where(left_half, packed[2:3], turned[3:4]),
        ],
        axis=0,
    )
    lists[me] = own_list
    to_group(0, lambda peer: lists.at[me], lists.at[me])
    for copy in local[1:]:
        copy.wait()

    def unpack(start, inside, targets):
        rows = slice(start, start + 8)
        put = slice(GUARD + start, GUARD + start + 8)
        for at in range(lane_tiles):
            lanes = slice(at * LANES, (at + 1) * LANES)
            parts = [state_ext[field, rows, lanes] for field in range(4)]
            if inside is not None:
                parts = [jnp.where(inside, part, 0.0) for part in parts]
            for target, target_rows in targets:
                for field in range(4):
                    target[field, at, target_rows, :] = parts[field]
            wet = wet_ext[rows, lanes].astype(F32)
            if inside is not None:
                wet = jnp.where(inside, wet, 0.0)
            wwork[at, put, :] = wet
            hwork[at, put, :] = depth_ext[rows, lanes]

    edge_starts = (0, ext_rows - strip)
    for start in range(HALO, HALO + grid_rows, 8):
        targets = [(work, slice(GUARD + start, GUARD + start + 8))]
        for side in range(2):
            at_row = start - edge_starts[side]
            if 0 <= at_row < strip:
                targets.append((edge.at[side], slice(GUARD + at_row, GUARD + at_row + 8)))
        unpack(start, None, targets)

    first_lane = iota((8, LANES), 1) == 0
    end_lane = iota((8, LANES), 1) == LANES - 1

    def across(parts):
        up = [pltpu.roll(part, LANES - 1, axis=1) for part in parts] + [nothing]
        down = [nothing] + [pltpu.roll(part, 1, axis=1) for part in parts]
        return [
            jnp.where(end_lane, up[at + 1], up[at])
            - jnp.where(first_lane, down[at], down[at + 1])
            for at in range(lane_tiles)
        ]

    def advance(fields, flux, cross, first, last, shift):
        for start in range(first, last, 8):
            rows = slice(start, start + 8)
            fixed = slice(start + shift, start + shift + 8)
            after = slice(start + 1, start + 9)
            before = slice(start - 1, start + 7)
            slope_y = across([fields[0, at, rows, :] for at in range(lane_tiles)])
            flow = []
            for at in range(lane_tiles):
                wet = wwork[at, fixed, :]
                height = hwork[at, fixed, :]
                slope_x = fields[0, at, after, :] - fields[0, at, before, :]
                new_x = wet * (FRICTION * fields[1, at, rows, :] - PRESSURE * slope_x)
                new_y = wet * (FRICTION * fields[2, at, rows, :] - PRESSURE * slope_y[at])
                fields[1, at, rows, :] = new_x
                fields[2, at, rows, :] = new_y
                flux[at, rows, :] = height * new_x
                flow.append(height * new_y)
            for at, part in enumerate(across(flow)):
                cross[at, rows, :] = part
        for start in range(last - 8, first - 8, -8):
            rows = slice(start, start + 8)
            fixed = slice(start + shift, start + shift + 8)
            after = slice(start + 1, start + 9)
            before = slice(start - 1, start + 7)
            for at in range(lane_tiles):
                wet = wwork[at, fixed, :]
                level = fields[0, at, rows, :]
                energy = fields[3, at, rows, :]
                spill = (flux[at, after, :] - flux[at, before, :]) + cross[at, rows, :]
                fields[0, at, rows, :] = wet * (level - DIVERGE * spill + FORCING * energy)
                fields[3, at, rows, :] = wet * (
                    energy - UPWIND * (energy - fields[3, at, before, :]) - DAMPING * energy
                )

    def inner_step(step, carry):
        advance(work, flux, cross, own_start, own_end, 0)
        return carry

    lax.fori_loop(0, STEPS, inner_step, 0)

    slab = 4 * lane_tiles
    edge_owners = HALO // 4

    def build(chunk, first, last):
        for field in range(2):
            for at in range(lane_tiles):
                for row in range(2):
                    slab_out[
                        chunk,
                        pl.ds(
                            first * slab + field * 8 + at * 2 + row, last - first, stride=slab
                        ),
                        :,
                    ] = work[
                        2 * chunk + field,
                        at,
                        pl.ds(own_start + 2 * first + row, last - first, stride=2),
                        :,
                    ]

    def slab_of(ref, chunk, owner):
        return ref.at[chunk, pl.ds(pl.multiple_of(owner * slab, slab), slab)]

    def send_slabs(chunk, first, last):
        count = last - first

        def one(step, carry):
            peer = first + lax.rem(me + step, count)

            @pl.when(peer != me)
            def _():
                send(2 + chunk, peer, slab_of(slab_out, chunk, peer), slab_of(slab_in, chunk, me))

            return carry

        lax.fori_loop(0, count, one, 0)

    if members > 2 * edge_owners:
        for chunk in range(2):
            build(chunk, edge_owners, members - edge_owners)
        send_slabs(0, edge_owners, members - edge_owners)

    for copy in halos:
        copy.wait_recv()
    for start in range(0, HALO, 8):
        unpack(start, tile > 0, [(edge.at[0], slice(GUARD + start, GUARD + start + 8))])
    for start in range(HALO + grid_rows, ext_rows, 8):
        at_row = start - edge_starts[1]
        unpack(
            start,
            tile < tiles - 1,
            [(edge.at[1], slice(GUARD + at_row, GUARD + at_row + 8))],
        )

    def edge_step(step, carry):
        for side in range(2):
            advance(
                edge.at[side],
                edge_flux.at[side],
                edge_cross.at[side],
                GUARD,
                GUARD + strip,
                edge_starts[side],
            )
        return carry

    lax.fori_loop(0, STEPS, edge_step, 0)
    for side in range(2):
        for start in (GUARD + 8, GUARD + 16):
            for field in range(4):
                for at in range(lane_tiles):
                    put = start + edge_starts[side]
                    work[field, at, put : put + 8, :] = edge[side, field, at, start : start + 8, :]

    first_line = TABLE_PAD - OBS_HALO // 2
    last_line = TABLE_PAD + own_table + OBS_HALO // 2
    offset = (cell_ext[...] & (SPACING - 1)).astype(BF16)
    place = iota((1, LANES), 1) & (SPACING - 1)
    chosen = [[], [], []]
    gathers = []
    for parity in range(2):
        for at in range(lane_tiles):
            owner = iota((LANES, LANES), 0) // SPACING + (parity * 64 + at * 16)
            gathers.append((owner == iota((LANES, LANES), 1)).astype(BF16))
            owner_t = iota((LANES, LANES), 1) // SPACING + (parity * 64 + at * 16)
            scatter = (owner_t == iota((LANES, LANES), 0)).astype(BF16)
            wanted = dot(offset, scatter).astype(jnp.int32) == place
            level = work[0, at, pl.ds(GUARD + parity, table_rows, stride=2), :]
            level = jnp.where(wanted, level, 0.0)
            high, _ = split(level)
            middle, low = split(level - high.astype(F32))
            for part, piece in zip(chosen, (high, middle, low)):
                part.append(piece)
    gather = jnp.concatenate(gathers, axis=0)
    pieces = [dot(jnp.concatenate(part, axis=1), gather) for part in chosen]
    table[...] = ((pieces[2] + pieces[1]) + pieces[0]) * gain_ext[...]

    group_done(group_recv, 0, lists, others)
    base = obs_tile - TABLE_PAD * LANES
    for start in range(0, members, 4):
        slots = jnp.concatenate([lists[start + i] for i in range(4)], axis=0) - base
        found = lookup(
            table, first_line, last_line, slots // LANES, slots & (LANES - 1)
        )
        for i in range(4):
            pick_out[start + i] = found[2 * i : 2 * i + 2, :]
    pick_in[me] = pick_out[me]
    to_group(1, lambda peer: pick_out.at[peer], pick_in.at[me])

    for chunk in range(2):
        build(chunk, 0, edge_owners)
        build(chunk, members - edge_owners, members)
    send_slabs(0, 0, edge_owners)
    send_slabs(0, members - edge_owners, members)
    send_slabs(1, 0, members)
    own_slab = pl.ds(pl.multiple_of(me * slab, slab), slab)
    for chunk in range(2):
        slab_in[chunk, own_slab, :] = slab_out[chunk, own_slab, :]

    names = jnp.concatenate([own_list] * 4, axis=0)
    slots = names - base
    high, low = slots // LANES, slots & (LANES - 1)
    value = lookup(value_ext, first_line, last_line, high, low)
    error = lookup(error_ext, first_line, last_line, high, low)
    value, error = value[0:2], error[0:2]
    row_index = me * 2 + iota((2, LANES), 0)
    centre = obs_tile + row_index * 64
    dist = (own_list - centre).astype(F32) / radius
    counts = raw_count[...]
    slot = iota((1, LANES), 1) & 63
    limit = jnp.concatenate(
        [
            jnp.where(
                left_half, counts[0:1, 2 * i : 2 * i + 1], counts[0:1, 2 * i + 1 : 2 * i + 2]
            )
            for i in range(2)
        ],
        axis=0,
    )
    live = slot < limit
    precision = jnp.where(live, 1.0 / ((1.0 + 4.0 * dist * dist) * error), 0.0)

    size = 4 * members
    patch_of_line = iota((size, 2 * LANES), 0) // members
    patch_of_slot = iota((size, 2 * LANES), 1) // 64
    line, column = iota((size, size), 0) // members, iota((size, size), 1) // members
    same = line == column
    diagonal = iota((members, size), 0) == iota((members, size), 1) % members
    eye = jnp.where(diagonal, 1.0, 0.0)
    ones = jnp.where(same, 1.0, 0.0).astype(BF16)
    patch_ones = (iota((2 * LANES, size), 0) // 64 == iota((2 * LANES, size), 1) // members)
    patch_ones = jnp.where(patch_ones, 1.0, 0.0).astype(BF16)

    def blocks(packed):
        return jnp.where(same, jnp.concatenate([packed] * 4, axis=0), 0.0)

    group_done(group_recv, 1, pick_in, others)
    picked = jnp.concatenate([pick_in[:, i, :] for i in range(2)], axis=1)
    mean_eq = jnp.sum(picked, axis=0, keepdims=True) * (1.0 / members)
    spread = picked - mean_eq
    precision = jnp.concatenate([precision[0:1], precision[1:2]], axis=1)
    value = jnp.concatenate([value[0:1], value[1:2]], axis=1)
    weighted = spread * precision
    by_patch = jnp.where(
        patch_of_line == patch_of_slot, jnp.concatenate([spread] * 4, axis=0), 0.0
    )
    gram = lax.dot_general(
        weighted, by_patch, (((1,), (1,)), ((), ())), precision=HIGH, preferred_element_type=F32
    )
    proj = exact_dot(weighted * (value - mean_eq), patch_ones)

    amat = gram + (members - 1.0) * eye
    trace = jnp.sum(exact_dot(jnp.where(diagonal, amat, 0.0), ones), axis=0, keepdims=True)

    def sweep(step, carry):
        current, inverse = carry
        factor = 1.5 * eye - 0.5 * dot3(inverse, blocks(current))
        return dot3(current, blocks(factor)), dot3(factor, blocks(inverse))

    current, inverse = lax.fori_loop(0, NS_ITERS, sweep, (amat / trace, eye))
    root = inverse / jnp.sqrt(trace)
    wbar = dot3(root, blocks(dot3(root, blocks(proj))))
    wtot = (members - 1.0) ** 0.5 * root + wbar
    mean = jnp.sum(wtot, axis=0, keepdims=True) * (1.0 / members)
    mix = jnp.transpose(blocks(wtot - mean + 1.0 / members))
    mix_high, mix_low = split(mix)
    mix_both = jnp.concatenate([mix_high, mix_low], axis=0)

    for chunk in range(2):
        group_done(group_recv, 2 + chunk, slab_in.at[chunk], others * slab)
        for field in range(2):
            lines = [
                [
                    slab_in[chunk, pl.ds(field * 8 + at * 2 + row, members, stride=slab), :]
                    for at in range(lane_tiles)
                ]
                for row in range(2)
            ]
            inputs = jnp.concatenate(
                [
                    jnp.concatenate(lines[row][2 * side : 2 * side + 2], axis=1)
                    for row in range(2)
                    for side in range(2)
                ],
                axis=0,
            )
            high, low = split(inputs)
            both = dot(mix_both, high)
            mixed = (both[size:] + dot(mix_high, low)) + both[:size]
            for row in range(2):
                for at in range(lane_tiles):
                    patch = row * 2 + at // 2
                    mix_out[
                        chunk, pl.ds(field * 8 + at * 2 + row, members, stride=slab), :
                    ] = mixed[
                        patch * members : (patch + 1) * members,
                        (at % 2) * LANES : (at % 2 + 1) * LANES,
                    ]
        back_in[chunk, own_slab, :] = mix_out[chunk, own_slab, :]
        to_group(
            4 + chunk,
            lambda peer: slab_of(mix_out, chunk, peer),
            back_in.at[chunk, own_slab],
        )
    for chunk in range(2):
        group_done(group_recv, 4 + chunk, back_in.at[chunk], others * slab)
        for field in range(2):
            for at in range(lane_tiles):
                for row in range(2):
                    rows_out[2 * chunk + field, at, pl.ds(row, members, stride=2), :] = back_in[
                        chunk, pl.ds(field * 8 + at * 2 + row, members, stride=slab), :
                    ]
        for field in range(2 * chunk, 2 * chunk + 2):
            for at in range(lane_tiles):
                out_ref[0, field, :, at * LANES : (at + 1) * LANES] = rows_out[field, at]

    for copy in halos:
        copy.wait_send()
    group_done(group_send, 0, lists, others)
    group_done(group_send, 1, pick_out, others)
    for chunk in range(2):
        group_done(group_send, 2 + chunk, slab_out.at[chunk], others * slab)
        group_done(group_send, 4 + chunk, mix_out.at[chunk], others * slab)


def body(
    realization_array,
    water_depth,
    wet_mask,
    obs_cell,
    obs_value,
    obs_error,
    celer_gain,
    obs_list,
    obs_count,
):
    members = lax.axis_size("member")
    tiles = lax.axis_size("tile")
    grid_rows, width = water_depth.shape
    ext_rows = grid_rows + 2 * HALO
    lane_tiles = width // LANES
    own_table = obs_cell.shape[0] // LANES
    table_rows = own_table + 2 * TABLE_PAD
    slab_rows = members * 4 * lane_tiles
    strip = 2 * HALO + 2 * GUARD
    deep = ext_rows + 2 * GUARD
    as_lines = lambda array: array.reshape(own_table, LANES)
    far = pl.BlockSpec(memory_space=pltpu.HBM)
    near = pl.BlockSpec(memory_space=pltpu.VMEM)
    return pl.pallas_call(
        functools.partial(kernel, members, tiles, grid_rows),
        out_shape=jax.ShapeDtypeStruct(realization_array.shape, F32),
        in_specs=[far] * 9,
        out_specs=near,
        scratch_shapes=[
            pltpu.VMEM((4, ext_rows, width), F32),
            pltpu.VMEM((ext_rows, width), F32),
            pltpu.VMEM((ext_rows, width), jnp.int32),
            pltpu.VMEM((table_rows, LANES), jnp.int32),
            pltpu.VMEM((table_rows, LANES), F32),
            pltpu.VMEM((table_rows, LANES), F32),
            pltpu.VMEM((table_rows, LANES), F32),
            pltpu.VMEM((4, lane_tiles, deep, LANES), F32),
            pltpu.VMEM((2, 4, lane_tiles, strip, LANES), F32),
            pltpu.VMEM((lane_tiles, deep, LANES), F32),
            pltpu.VMEM((lane_tiles, deep, LANES), F32),
            pltpu.VMEM((lane_tiles, deep, LANES), F32),
            pltpu.VMEM((lane_tiles, deep, LANES), F32),
            pltpu.VMEM((2, lane_tiles, strip, LANES), F32),
            pltpu.VMEM((2, lane_tiles, strip, LANES), F32),
            pltpu.VMEM(obs_list.shape[1:], jnp.int32),
            pltpu.VMEM(obs_count.shape, jnp.int32),
            pltpu.VMEM((8, LANES), jnp.int32),
            pltpu.VMEM((members, 2, LANES), jnp.int32),
            pltpu.VMEM((table_rows, LANES), F32),
            pltpu.VMEM((members, 2, LANES), F32),
            pltpu.VMEM((members, 2, LANES), F32),
            pltpu.VMEM((2, slab_rows, LANES), F32),
            pltpu.VMEM((2, slab_rows, LANES), F32),
            pltpu.VMEM((2, slab_rows, LANES), F32),
            pltpu.VMEM((2, slab_rows, LANES), F32),
            pltpu.VMEM((4, lane_tiles, grid_rows, LANES), F32),
            pltpu.SemaphoreType.DMA((9,)),
            pltpu.SemaphoreType.DMA((2, 7)),
            pltpu.SemaphoreType.DMA((2, 7)),
            pltpu.SemaphoreType.DMA((6,)),
            pltpu.SemaphoreType.DMA((6,)),
        ],
        compiler_params=pltpu.CompilerParams(
            collective_id=0, has_side_effects=True, vmem_limit_bytes=32 * 1024 * 1024
        ),
    )(
        *[
            pltpu.with_memory_space_constraint(array, pltpu.HBM)
            for array in (
                realization_array,
                water_depth,
                wet_mask,
                as_lines(obs_cell),
                as_lines(celer_gain),
                as_lines(obs_value),
                as_lines(obs_error),
                obs_list,
                obs_count,
            )
        ]
    )


def solution(mesh):
    return jax.shard_map(
        body,
        mesh=mesh,
        in_specs=(
            P("member", None, "tile", None),
            P("tile", None),
            P("tile", None),
            P("tile"),
            P("tile"),
            P("tile"),
            P("tile"),
            P("tile", "member", None),
            P("tile", "member"),
        ),
        out_specs=P("member", None, "tile", None),
        check_vma=False,
    )
```

```python
import functools

import jax
import jax.numpy as jnp
from jax import lax
from jax.experimental import pallas as pl
from jax.experimental.pallas import tpu as pltpu
from jax.sharding import PartitionSpec as P

MESH = pl.DeviceIdType.MESH
HIGH = lax.Precision.HIGHEST
F32 = jnp.float32
BF16 = jnp.bfloat16

REGION_POINTS = 256
OUTWARD = ((0, 1), (2, 3))
BACK = ((0,), (1,), (2, 3))
STEPS = 4
NS_ITERS = 14
SPACING = 8

FRICTION = 0.98
PRESSURE = 0.25
DIVERGE = 0.25
FORCING = 0.05
UPWIND = 0.4
DAMPING = 0.02

LANES = 128
GUARD = 8
HALO = 16
OBS_HALO = 8
TABLE_PAD = 8


def iota(shape, dim):
    return lax.broadcasted_iota(jnp.int32, shape, dim)


def dot(left, right, precision=None):
    return lax.dot_general(
        left, right, (((1,), (0,)), ((), ())), precision=precision, preferred_element_type=F32
    )


def split(x):
    high = x.astype(BF16)
    return high, (x - high.astype(F32)).astype(BF16)


def split3(x):
    high, _ = split(x)
    middle, low = split(x - high.astype(F32))
    return high, middle, low


def dot6(left, right):
    left_high, left_middle, left_low = split3(left)
    right_high, right_middle, right_low = split3(right)
    rows = left.shape[0]
    first = dot(jnp.concatenate([left_high, left_middle, left_low], axis=0), right_high)
    second = dot(jnp.concatenate([left_high, left_middle], axis=0), right_middle)
    third = dot(left_high, right_low)
    small = first[2 * rows :] + second[rows:] + third
    return (small + (first[rows : 2 * rows] + second[:rows])) + first[:rows]


def exact_dot(left, ones):
    rows = left.shape[0]
    parts = dot(jnp.concatenate(split3(left), axis=0), ones)
    return (parts[2 * rows :] + parts[rows : 2 * rows]) + parts[:rows]


def lookup(table, first, last, high, low):
    found = jnp.zeros(high.shape, table.dtype)
    for row in range(first, last):
        line = jnp.broadcast_to(table[row : row + 1, :], high.shape)
        found = jnp.where(
            high == row,
            jnp.take_along_axis(line, low, axis=1, mode="promise_in_bounds"),
            found,
        )
    return found


def kernel(
    members,
    tiles,
    grid_rows,
    state_ref,
    depth_ref,
    wet_ref,
    cell_ref,
    gain_ref,
    value_ref,
    error_ref,
    list_ref,
    count_ref,
    out_ref,
    state_ext,
    depth_ext,
    wet_ext,
    cell_ext,
    gain_ext,
    value_ext,
    error_ext,
    work,
    edge,
    hwork,
    wwork,
    flux,
    cross,
    edge_flux,
    edge_cross,
    raw_list,
    raw_count,
    pack,
    lists,
    table,
    pick_out,
    pick_in,
    slab_out,
    slab_in,
    mix_out,
    back_in,
    rows_out,
    local_sem,
    halo_send,
    halo_recv,
    group_send,
    group_recv,
):
    me = lax.axis_index("member")
    tile = lax.axis_index("tile")
    above = lax.rem(tile + tiles - 1, tiles)
    below = lax.rem(tile + 1, tiles)
    ext_rows = grid_rows + 2 * HALO
    lane_tiles = 4
    obs_tile = grid_rows * 64
    radius = obs_tile // 8
    own_table = obs_tile // LANES
    table_rows = own_table + 2 * TABLE_PAD
    others = members - 1

    barrier = pltpu.get_barrier_semaphore()

    def greet(step, carry):
        peer = lax.rem(me + step, members)
        pl.semaphore_signal(barrier, inc=1, device_id={"member": peer}, device_id_type=MESH)
        return carry

    pl.semaphore_signal(barrier, inc=1, device_id={"tile": above}, device_id_type=MESH)
    pl.semaphore_signal(barrier, inc=1, device_id={"tile": below}, device_id_type=MESH)
    lax.fori_loop(1, members, greet, 0)

    own_rows = pl.ds(HALO, grid_rows)
    own_lines = pl.ds(TABLE_PAD, own_table)
    tables = (
        (cell_ref, cell_ext),
        (gain_ref, gain_ext),
        (value_ref, value_ext),
        (error_ref, error_ext),
    )
    pairs = [
        (list_ref.at[0], raw_list),
        (count_ref, raw_count),
        (state_ref.at[0], state_ext.at[:, own_rows]),
        (depth_ref, depth_ext.at[own_rows]),
        (wet_ref, wet_ext.at[own_rows]),
    ] + [(ref, ext.at[own_lines]) for ref, ext in tables]
    local = [
        pltpu.make_async_copy(source, destination, local_sem.at[i])
        for i, (source, destination) in enumerate(pairs)
    ]
    for copy in local:
        copy.start()

    nothing = jnp.zeros((8, LANES), F32)
    strip = 2 * HALO
    own_start = GUARD + HALO
    own_end = own_start + grid_rows
    for at in range(lane_tiles):
        for field in (0, 3):
            work[field, at, own_start - 8 : own_start, :] = nothing
            work[field, at, own_end : own_end + 8, :] = nothing
            for side in range(2):
                edge[side, field, at, 0:GUARD, :] = nothing
                edge[side, field, at, GUARD + strip :, :] = nothing
        flux[at, own_start - 8 : own_start, :] = nothing
        flux[at, own_end : own_end + 8, :] = nothing
        for side in range(2):
            edge_flux[side, at, 0:GUARD, :] = nothing
            edge_flux[side, at, GUARD + strip :, :] = nothing
    pack[...] = jnp.zeros(pack.shape, jnp.int32)

    local[0].wait()
    pack[0:4, 0:64] = raw_list[...]
    packed = pack[...]
    turned = pltpu.roll(packed, 64, axis=1)
    left_half = iota((1, LANES), 1) < 64
    own_list = jnp.concatenate(
        [
            jnp.where(left_half, packed[0:1], turned[1:2]),
            jnp.where(left_half, packed[2:3], turned[3:4]),
        ],
        axis=0,
    )
    lists[me] = own_list
    for copy in local[1:]:
        copy.wait()

    def unpack(start, inside, targets):
        rows = slice(start, start + 8)
        put = slice(GUARD + start, GUARD + start + 8)
        for at in range(lane_tiles):
            lanes = slice(at * LANES, (at + 1) * LANES)
            parts = [state_ext[field, rows, lanes] for field in range(4)]
            if inside is not None:
                parts = [jnp.where(inside, part, 0.0) for part in parts]
            for target, target_rows in targets:
                for field in range(4):
                    target[field, at, target_rows, :] = parts[field]
            wet = wet_ext[rows, lanes].astype(F32)
            if inside is not None:
                wet = jnp.where(inside, wet, 0.0)
            wwork[at, put, :] = wet
            hwork[at, put, :] = depth_ext[rows, lanes]

    edge_starts = (0, ext_rows - strip)
    for start in range(HALO, HALO + grid_rows, 8):
        targets = [(work, slice(GUARD + start, GUARD + start + 8))]
        for side in range(2):
            at_row = start - edge_starts[side]
            if 0 <= at_row < strip:
                targets.append((edge.at[side], slice(GUARD + at_row, GUARD + at_row + 8)))
        unpack(start, None, targets)

    first_lane = iota((8, LANES), 1) == 0
    end_lane = iota((8, LANES), 1) == LANES - 1

    def across(parts):
        up = [pltpu.roll(part, LANES - 1, axis=1) for part in parts] + [nothing]
        down = [nothing] + [pltpu.roll(part, 1, axis=1) for part in parts]
        return [
            jnp.where(end_lane, up[at + 1], up[at])
            - jnp.where(first_lane, down[at], down[at + 1])
            for at in range(lane_tiles)
        ]

    def advance(fields, flux, cross, first, last, shift):
        for start in range(first, last, 8):
            rows = slice(start, start + 8)
            fixed = slice(start + shift, start + shift + 8)
            after = slice(start + 1, start + 9)
            before = slice(start - 1, start + 7)
            slope_y = across([fields[0, at, rows, :] for at in range(lane_tiles)])
            flow = []
            for at in range(lane_tiles):
                wet = wwork[at, fixed, :]
                height = hwork[at, fixed, :]
                slope_x = fields[0, at, after, :] - fields[0, at, before, :]
                new_x = wet * (FRICTION * fields[1, at, rows, :] - PRESSURE * slope_x)
                new_y = wet * (FRICTION * fields[2, at, rows, :] - PRESSURE * slope_y[at])
                fields[1, at, rows, :] = new_x
                fields[2, at, rows, :] = new_y
                flux[at, rows, :] = height * new_x
                flow.append(height * new_y)
            for at, part in enumerate(across(flow)):
                cross[at, rows, :] = part
        for start in range(last - 8, first - 8, -8):
            rows = slice(start, start + 8)
            fixed = slice(start + shift, start + shift + 8)
            after = slice(start + 1, start + 9)
            before = slice(start - 1, start + 7)
            for at in range(lane_tiles):
                wet = wwork[at, fixed, :]
                level = fields[0, at, rows, :]
                energy = fields[3, at, rows, :]
                spill = (flux[at, after, :] - flux[at, before, :]) + cross[at, rows, :]
                fields[0, at, rows, :] = wet * (level - DIVERGE * spill + FORCING * energy)
                fields[3, at, rows, :] = wet * (
                    energy - UPWIND * (energy - fields[3, at, before, :]) - DAMPING * energy
                )

    def inner_step(step, carry):
        advance(work, flux, cross, own_start, own_end, 0)
        return carry

    pl.semaphore_wait(barrier, others + 2)

    halos = []
    for way, (target, source_row, target_row, source_line, target_line) in enumerate(
        (
            (below, grid_rows - HALO, 0, own_table - TABLE_PAD, 0),
            (above, 0, HALO + grid_rows, 0, TABLE_PAD + own_table),
        )
    ):
        source_rows, target_rows = pl.ds(source_row, HALO), pl.ds(target_row, HALO)
        source_lines, target_lines = pl.ds(source_line, TABLE_PAD), pl.ds(target_line, TABLE_PAD)
        pairs = [
            (state_ref.at[0, :, source_rows], state_ext.at[:, target_rows]),
            (depth_ref.at[source_rows], depth_ext.at[target_rows]),
            (wet_ref.at[source_rows], wet_ext.at[target_rows]),
        ] + [(ref.at[source_lines], ext.at[target_lines]) for ref, ext in tables]
        for i, (source, destination) in enumerate(pairs):
            copy = pltpu.make_async_remote_copy(
                src_ref=source,
                dst_ref=destination,
                send_sem=halo_send.at[way, i],
                recv_sem=halo_recv.at[way, i],
                device_id={"tile": target},
                device_id_type=MESH,
            )
            copy.start()
            halos.append(copy)

    def send(which, peer, source, destination):
        pltpu.make_async_remote_copy(
            src_ref=source,
            dst_ref=destination,
            send_sem=group_send.at[which],
            recv_sem=group_recv.at[which],
            device_id={"member": peer},
            device_id_type=MESH,
        ).start()

    def to_group(which, source, destination):
        def one(step, carry):
            peer = lax.rem(me + step, members)
            send(which, peer, source(peer), destination)
            return carry

        lax.fori_loop(1, members, one, 0)

    def group_done(sems, which, ref, size):
        part = ref.at[pl.ds(0, size)]
        pltpu.make_async_copy(part, part, sems.at[which]).wait()

    to_group(0, lambda peer: lists.at[me], lists.at[me])
    lax.fori_loop(0, STEPS, inner_step, 0)

    slab = 2 * lane_tiles
    edge_owners = HALO // 4

    def build(field, first, last):
        for at in range(lane_tiles):
            for row in range(2):
                slab_out[
                    field, pl.ds(first * slab + at * 2 + row, last - first, stride=slab), :
                ] = work[
                    field, at, pl.ds(own_start + 2 * first + row, last - first, stride=2), :
                ]

    def slab_of(ref, fields, owner):
        return ref.at[
            pl.ds(fields[0], len(fields)), pl.ds(pl.multiple_of(owner * slab, slab), slab)
        ]

    def slabs_done(sems, which, ref, fields):
        part = ref.at[pl.ds(fields[0], len(fields)), pl.ds(0, others * slab)]
        pltpu.make_async_copy(part, part, sems.at[which]).wait()

    def send_slabs(chunk, first, last):
        count = last - first

        def one(step, carry):
            peer = first + lax.rem(me + step, count)

            @pl.when(peer != me)
            def _():
                fields = OUTWARD[chunk]
                send(2 + chunk, peer, slab_of(slab_out, fields, peer), slab_of(slab_in, fields, me))

            return carry

        lax.fori_loop(0, count, one, 0)

    if members > 2 * edge_owners:
        for field in range(4):
            build(field, edge_owners, members - edge_owners)
        send_slabs(0, edge_owners, members - edge_owners)

    for copy in halos:
        copy.wait_recv()
    for start in range(0, HALO, 8):
        unpack(start, tile > 0, [(edge.at[0], slice(GUARD + start, GUARD + start + 8))])
    for start in range(HALO + grid_rows, ext_rows, 8):
        at_row = start - edge_starts[1]
        unpack(
            start,
            tile < tiles - 1,
            [(edge.at[1], slice(GUARD + at_row, GUARD + at_row + 8))],
        )

    def edge_step(step, carry):
        for side in range(2):
            advance(
                edge.at[side],
                edge_flux.at[side],
                edge_cross.at[side],
                GUARD,
                GUARD + strip,
                edge_starts[side],
            )
        return carry

    lax.fori_loop(0, STEPS, edge_step, 0)
    for side in range(2):
        for start in (GUARD + 8, GUARD + 16):
            for field in range(4):
                for at in range(lane_tiles):
                    put = start + edge_starts[side]
                    work[field, at, put : put + 8, :] = edge[side, field, at, start : start + 8, :]

    first_line = TABLE_PAD - OBS_HALO // 2
    last_line = TABLE_PAD + own_table + OBS_HALO // 2
    offset = (cell_ext[...] & (SPACING - 1)).astype(BF16)
    place = iota((1, LANES), 1) & (SPACING - 1)
    chosen = [[], [], []]
    gathers = []
    for parity in range(2):
        for at in range(lane_tiles):
            owner = iota((LANES, LANES), 0) // SPACING + (parity * 64 + at * 16)
            gathers.append((owner == iota((LANES, LANES), 1)).astype(BF16))
            owner_t = iota((LANES, LANES), 1) // SPACING + (parity * 64 + at * 16)
            scatter = (owner_t == iota((LANES, LANES), 0)).astype(BF16)
            wanted = dot(offset, scatter).astype(jnp.int32) == place
            level = work[0, at, pl.ds(GUARD + parity, table_rows, stride=2), :]
            level = jnp.where(wanted, level, 0.0)
            for part, piece in zip(chosen, split3(level)):
                part.append(piece)
    gather = jnp.concatenate(gathers, axis=0)
    pieces = [dot(jnp.concatenate(part, axis=1), gather) for part in chosen]
    table[...] = ((pieces[2] + pieces[1]) + pieces[0]) * gain_ext[...]

    group_done(group_recv, 0, lists, others)
    base = obs_tile - TABLE_PAD * LANES
    for start in range(0, members, 4):
        slots = jnp.concatenate([lists[start + i] for i in range(4)], axis=0) - base
        found = lookup(
            table, first_line, last_line, slots // LANES, slots & (LANES - 1)
        )
        for i in range(4):
            pick_out[start + i] = found[2 * i : 2 * i + 2, :]
    pick_in[me] = pick_out[me]
    to_group(1, lambda peer: pick_out.at[peer], pick_in.at[me])

    for field in range(4):
        build(field, 0, edge_owners)
        build(field, members - edge_owners, members)
    send_slabs(0, 0, edge_owners)
    send_slabs(0, members - edge_owners, members)
    send_slabs(1, 0, members)
    own_slab = pl.ds(pl.multiple_of(me * slab, slab), slab)
    for field in range(4):
        slab_in[field, own_slab, :] = slab_out[field, own_slab, :]

    names = jnp.concatenate([own_list] * 4, axis=0)
    slots = names - base
    high, low = slots // LANES, slots & (LANES - 1)
    value = lookup(value_ext, first_line, last_line, high, low)
    error = lookup(error_ext, first_line, last_line, high, low)
    value, error = value[0:2], error[0:2]
    row_index = me * 2 + iota((2, LANES), 0)
    centre = obs_tile + row_index * 64
    dist = (own_list - centre).astype(F32) / radius
    counts = raw_count[...]
    slot = iota((1, LANES), 1) & 63
    limit = jnp.concatenate(
        [
            jnp.where(
                left_half, counts[0:1, 2 * i : 2 * i + 1], counts[0:1, 2 * i + 1 : 2 * i + 2]
            )
            for i in range(2)
        ],
        axis=0,
    )
    live = slot < limit
    precision = jnp.where(live, 1.0 / ((1.0 + 4.0 * dist * dist) * error), 0.0)

    size = 4 * members
    patch_of_line = iota((size, 2 * LANES), 0) // members
    patch_of_slot = iota((size, 2 * LANES), 1) // 64
    line, column = iota((size, size), 0) // members, iota((size, size), 1) // members
    same = line == column
    diagonal = iota((members, size), 0) == iota((members, size), 1) % members
    eye = jnp.where(diagonal, 1.0, 0.0)
    patch_ones = (iota((2 * LANES, size), 0) // 64 == iota((2 * LANES, size), 1) // members)
    patch_ones = jnp.where(patch_ones, 1.0, 0.0).astype(BF16)

    def blocks(packed):
        return jnp.where(same, jnp.concatenate([packed] * 4, axis=0), 0.0)

    group_done(group_recv, 1, pick_in, others)
    picked = jnp.concatenate([pick_in[:, i, :] for i in range(2)], axis=1)
    mean_eq = jnp.sum(picked, axis=0, keepdims=True) * (1.0 / members)
    spread = picked - mean_eq
    precision = jnp.concatenate([precision[0:1], precision[1:2]], axis=1)
    value = jnp.concatenate([value[0:1], value[1:2]], axis=1)
    weighted = spread * precision
    by_patch = jnp.where(
        patch_of_line == patch_of_slot, jnp.concatenate([spread] * 4, axis=0), 0.0
    )
    gram = lax.dot_general(
        weighted, by_patch, (((1,), (1,)), ((), ())), precision=HIGH, preferred_element_type=F32
    )
    sums = exact_dot(
        jnp.concatenate([weighted * (value - mean_eq), weighted * spread], axis=0), patch_ones
    )
    proj = sums[:members]
    trace = jnp.sum(sums[members:], axis=0, keepdims=True) + (members - 1.0) * members

    amat = gram + (members - 1.0) * eye

    def times(left, right):
        return dot6(left, blocks(right))

    def two_steps(square):
        second = times(square, square)
        third, fourth = times(second, square), times(second, second)
        after = 2.25 * square - 1.5 * second + 0.25 * third
        both = 2.25 * second - 1.5 * third + 0.25 * fourth
        return second, 2.25 * eye - 0.75 * (after + square) + 0.25 * both

    def three_steps(step, carry):
        square, inverse = carry
        second, factor = two_steps(square)
        once, twice = times(square, factor), times(second, factor)
        squared = times(factor, factor)
        product = 1.5 * factor - 0.5 * times(once, squared)
        moved = 1.5 * once - 0.5 * times(twice, squared)
        return times(moved, product), times(product, inverse)

    square, inverse = lax.fori_loop(0, (NS_ITERS - 2) // 3, three_steps, (amat / trace, eye))
    scale = 1.0 / jnp.sqrt(trace)
    early = times(inverse, proj)
    _, factor = two_steps(square)
    inverse = times(factor, inverse)
    wbar = times(inverse, times(factor, early)) / trace
    wtot = (members - 1.0) ** 0.5 * (inverse * scale) + wbar
    mean = jnp.sum(wtot, axis=0, keepdims=True) * (1.0 / members)
    mix = jnp.transpose(blocks(wtot - mean + 1.0 / members))
    mix_high, mix_low = split(mix)
    mix_both = jnp.concatenate([mix_high, mix_low], axis=0)

    for chunk, fields in enumerate(BACK):
        for field in fields:
            for coming, arriving in enumerate(OUTWARD):
                if field == arriving[0]:
                    slabs_done(group_recv, 2 + coming, slab_in, arriving)
            lines = [
                [
                    slab_in[field, pl.ds(at * 2 + row, members, stride=slab), :]
                    for at in range(lane_tiles)
                ]
                for row in range(2)
            ]
            inputs = jnp.concatenate(
                [
                    jnp.concatenate(lines[row][2 * side : 2 * side + 2], axis=1)
                    for row in range(2)
                    for side in range(2)
                ],
                axis=0,
            )
            high, low = split(inputs)
            both = dot(mix_both, high)
            mixed = (both[size:] + dot(mix_high, low)) + both[:size]
            for row in range(2):
                for at in range(lane_tiles):
                    patch = row * 2 + at // 2
                    mix_out[field, pl.ds(at * 2 + row, members, stride=slab), :] = mixed[
                        patch * members : (patch + 1) * members,
                        (at % 2) * LANES : (at % 2 + 1) * LANES,
                    ]
            back_in[field, own_slab, :] = mix_out[field, own_slab, :]
        to_group(
            4 + chunk,
            lambda peer: slab_of(mix_out, fields, peer),
            slab_of(back_in, fields, me),
        )
    for chunk, fields in enumerate(BACK):
        slabs_done(group_recv, 4 + chunk, back_in, fields)
        for field in fields:
            for at in range(lane_tiles):
                for row in range(2):
                    rows_out[field, at, pl.ds(row, members, stride=2), :] = back_in[
                        field, pl.ds(at * 2 + row, members, stride=slab), :
                    ]
        for field in fields:
            for at in range(lane_tiles):
                out_ref[0, field, :, at * LANES : (at + 1) * LANES] = rows_out[field, at]

    for copy in halos:
        copy.wait_send()
    group_done(group_send, 0, lists, others)
    group_done(group_send, 1, pick_out, others)
    for chunk, fields in enumerate(OUTWARD):
        slabs_done(group_send, 2 + chunk, slab_out, fields)
    for chunk, fields in enumerate(BACK):
        slabs_done(group_send, 4 + chunk, mix_out, fields)


def body(
    realization_array,
    water_depth,
    wet_mask,
    obs_cell,
    obs_value,
    obs_error,
    celer_gain,
    obs_list,
    obs_count,
):
    members = lax.axis_size("member")
    tiles = lax.axis_size("tile")
    grid_rows, width = water_depth.shape
    ext_rows = grid_rows + 2 * HALO
    lane_tiles = width // LANES
    own_table = obs_cell.shape[0] // LANES
    table_rows = own_table + 2 * TABLE_PAD
    slab_rows = members * 2 * lane_tiles
    strip = 2 * HALO + 2 * GUARD
    deep = ext_rows + 2 * GUARD
    as_lines = lambda array: array.reshape(own_table, LANES)
    far = pl.BlockSpec(memory_space=pltpu.HBM)
    near = pl.BlockSpec(memory_space=pltpu.VMEM)
    return pl.pallas_call(
        functools.partial(kernel, members, tiles, grid_rows),
        out_shape=jax.ShapeDtypeStruct(realization_array.shape, F32),
        in_specs=[far] * 9,
        out_specs=near,
        scratch_shapes=[
            pltpu.VMEM((4, ext_rows, width), F32),
            pltpu.VMEM((ext_rows, width), F32),
            pltpu.VMEM((ext_rows, width), jnp.int32),
            pltpu.VMEM((table_rows, LANES), jnp.int32),
            pltpu.VMEM((table_rows, LANES), F32),
            pltpu.VMEM((table_rows, LANES), F32),
            pltpu.VMEM((table_rows, LANES), F32),
            pltpu.VMEM((4, lane_tiles, deep, LANES), F32),
            pltpu.VMEM((2, 4, lane_tiles, strip, LANES), F32),
            pltpu.VMEM((lane_tiles, deep, LANES), F32),
            pltpu.VMEM((lane_tiles, deep, LANES), F32),
            pltpu.VMEM((lane_tiles, deep, LANES), F32),
            pltpu.VMEM((lane_tiles, deep, LANES), F32),
            pltpu.VMEM((2, lane_tiles, strip, LANES), F32),
            pltpu.VMEM((2, lane_tiles, strip, LANES), F32),
            pltpu.VMEM(obs_list.shape[1:], jnp.int32),
            pltpu.VMEM(obs_count.shape, jnp.int32),
            pltpu.VMEM((8, LANES), jnp.int32),
            pltpu.VMEM((members, 2, LANES), jnp.int32),
            pltpu.VMEM((table_rows, LANES), F32),
            pltpu.VMEM((members, 2, LANES), F32),
            pltpu.VMEM((members, 2, LANES), F32),
            pltpu.VMEM((4, slab_rows, LANES), F32),
            pltpu.VMEM((4, slab_rows, LANES), F32),
            pltpu.VMEM((4, slab_rows, LANES), F32),
            pltpu.VMEM((4, slab_rows, LANES), F32),
            pltpu.VMEM((4, lane_tiles, grid_rows, LANES), F32),
            pltpu.SemaphoreType.DMA((9,)),
            pltpu.SemaphoreType.DMA((2, 7)),
            pltpu.SemaphoreType.DMA((2, 7)),
            pltpu.SemaphoreType.DMA((4 + len(BACK),)),
            pltpu.SemaphoreType.DMA((4 + len(BACK),)),
        ],
        compiler_params=pltpu.CompilerParams(
            collective_id=0, has_side_effects=True, vmem_limit_bytes=32 * 1024 * 1024
        ),
    )(
        *[
            pltpu.with_memory_space_constraint(array, pltpu.HBM)
            for array in (
                realization_array,
                water_depth,
                wet_mask,
                as_lines(obs_cell),
                as_lines(celer_gain),
                as_lines(obs_value),
                as_lines(obs_error),
                obs_list,
                obs_count,
            )
        ]
    )


def solution(mesh):
    return jax.shard_map(
        body,
        mesh=mesh,
        in_specs=(
            P("member", None, "tile", None),
            P("tile", None),
            P("tile", None),
            P("tile"),
            P("tile"),
            P("tile"),
            P("tile"),
            P("tile", "member", None),
            P("tile", "member"),
        ),
        out_specs=P("member", None, "tile", None),
        check_vma=False,
    )
```

```python
import functools

import jax
import jax.numpy as jnp
from jax import lax
from jax.experimental import pallas as pl
from jax.experimental.pallas import tpu as pltpu
from jax.sharding import PartitionSpec as P

MESH = pl.DeviceIdType.MESH
HIGH = lax.Precision.HIGHEST
F32 = jnp.float32
BF16 = jnp.bfloat16

REGION_POINTS = 256
OUTWARD = ((0, 1), (2, 3))
BACK = ((0,), (1,), (2, 3))
STEPS = 4
NS_ITERS = 14
SPACING = 8

FRICTION = 0.98
PRESSURE = 0.25
DIVERGE = 0.25
FORCING = 0.05
UPWIND = 0.4
DAMPING = 0.02

LANES = 128
GUARD = 8
HALO = 16
OBS_HALO = 8
TABLE_PAD = 8


def iota(shape, dim):
    return lax.broadcasted_iota(jnp.int32, shape, dim)


def dot(left, right, precision=None):
    return lax.dot_general(
        left, right, (((1,), (0,)), ((), ())), precision=precision, preferred_element_type=F32
    )


def split(x):
    high = x.astype(BF16)
    return high, (x - high.astype(F32)).astype(BF16)


def split3(x):
    high, _ = split(x)
    middle, low = split(x - high.astype(F32))
    return high, middle, low


def dot6(left, right):
    left_high, left_middle, left_low = split3(left)
    right_high, right_middle, right_low = split3(right)
    rows = left.shape[0]
    straight = jnp.concatenate([left_high, left_middle], axis=1)
    crossed = jnp.concatenate([left_middle, left_high], axis=1)
    large = dot(
        jnp.concatenate([straight, crossed], axis=0),
        jnp.concatenate([right_high, right_middle], axis=0),
    )
    small = dot(
        jnp.concatenate([left_low, left_high], axis=1),
        jnp.concatenate([right_high, right_low], axis=0),
    )
    return (small + large[rows:]) + large[:rows]


def exact_dot(left, ones):
    rows = left.shape[0]
    parts = dot(jnp.concatenate(split3(left), axis=0), ones)
    return (parts[2 * rows :] + parts[rows : 2 * rows]) + parts[:rows]


def lookup(table, first, last, high, low):
    found = jnp.zeros(high.shape, table.dtype)
    for row in range(first, last):
        line = jnp.broadcast_to(table[row : row + 1, :], high.shape)
        found = jnp.where(
            high == row,
            jnp.take_along_axis(line, low, axis=1, mode="promise_in_bounds"),
            found,
        )
    return found


def kernel(
    members,
    tiles,
    grid_rows,
    state_ref,
    depth_ref,
    wet_ref,
    cell_ref,
    gain_ref,
    value_ref,
    error_ref,
    list_ref,
    count_ref,
    out_ref,
    state_ext,
    depth_ext,
    wet_ext,
    cell_ext,
    gain_ext,
    value_ext,
    error_ext,
    work,
    edge,
    hwork,
    wwork,
    flux,
    cross,
    edge_flux,
    edge_cross,
    raw_list,
    raw_count,
    pack,
    lists,
    table,
    pick_out,
    pick_in,
    slab_out,
    slab_in,
    mix_out,
    back_in,
    local_sem,
    halo_send,
    halo_recv,
    group_send,
    group_recv,
):
    me = lax.axis_index("member")
    tile = lax.axis_index("tile")
    above = lax.rem(tile + tiles - 1, tiles)
    below = lax.rem(tile + 1, tiles)
    ext_rows = grid_rows + 2 * HALO
    lane_tiles = 4
    obs_tile = grid_rows * 64
    radius = obs_tile // 8
    own_table = obs_tile // LANES
    table_rows = own_table + 2 * TABLE_PAD
    others = members - 1

    barrier = pltpu.get_barrier_semaphore()

    def greet(step, carry):
        peer = lax.rem(me + step, members)
        pl.semaphore_signal(barrier, inc=1, device_id={"member": peer}, device_id_type=MESH)
        return carry

    pl.semaphore_signal(barrier, inc=1, device_id={"tile": above}, device_id_type=MESH)
    pl.semaphore_signal(barrier, inc=1, device_id={"tile": below}, device_id_type=MESH)
    lax.fori_loop(1, members, greet, 0)

    own_rows = pl.ds(HALO, grid_rows)
    own_lines = pl.ds(TABLE_PAD, own_table)
    tables = (
        (cell_ref, cell_ext),
        (gain_ref, gain_ext),
        (value_ref, value_ext),
        (error_ref, error_ext),
    )
    pairs = [
        (list_ref.at[0], raw_list),
        (count_ref, raw_count),
        (state_ref.at[0], state_ext.at[:, own_rows]),
        (depth_ref, depth_ext.at[own_rows]),
        (wet_ref, wet_ext.at[own_rows]),
    ] + [(ref, ext.at[own_lines]) for ref, ext in tables]
    local = [
        pltpu.make_async_copy(source, destination, local_sem.at[i])
        for i, (source, destination) in enumerate(pairs)
    ]
    for copy in local:
        copy.start()

    nothing = jnp.zeros((8, LANES), F32)
    strip = 2 * HALO
    own_start = GUARD + HALO
    own_end = own_start + grid_rows
    for at in range(lane_tiles):
        for field in (0, 3):
            work[field, at, own_start - 8 : own_start, :] = nothing
            work[field, at, own_end : own_end + 8, :] = nothing
            for side in range(2):
                edge[side, field, at, 0:GUARD, :] = nothing
                edge[side, field, at, GUARD + strip :, :] = nothing
        flux[at, own_start - 8 : own_start, :] = nothing
        flux[at, own_end : own_end + 8, :] = nothing
        for side in range(2):
            edge_flux[side, at, 0:GUARD, :] = nothing
            edge_flux[side, at, GUARD + strip :, :] = nothing
    pack[...] = jnp.zeros(pack.shape, jnp.int32)

    local[0].wait()
    pack[0:4, 0:64] = raw_list[...]
    packed = pack[...]
    turned = pltpu.roll(packed, 64, axis=1)
    left_half = iota((1, LANES), 1) < 64
    own_list = jnp.concatenate(
        [
            jnp.where(left_half, packed[0:1], turned[1:2]),
            jnp.where(left_half, packed[2:3], turned[3:4]),
        ],
        axis=0,
    )
    lists[me] = own_list
    for copy in local[1:]:
        copy.wait()

    def unpack(start, inside, targets):
        rows = slice(start, start + 8)
        put = slice(GUARD + start, GUARD + start + 8)
        for at in range(lane_tiles):
            lanes = slice(at * LANES, (at + 1) * LANES)
            parts = [state_ext[field, rows, lanes] for field in range(4)]
            if inside is not None:
                parts = [jnp.where(inside, part, 0.0) for part in parts]
            for target, target_rows in targets:
                for field in range(4):
                    target[field, at, target_rows, :] = parts[field]
            wet = wet_ext[rows, lanes].astype(F32)
            if inside is not None:
                wet = jnp.where(inside, wet, 0.0)
            wwork[at, put, :] = wet
            hwork[at, put, :] = depth_ext[rows, lanes]

    edge_starts = (0, ext_rows - strip)
    for start in range(HALO, HALO + grid_rows, 8):
        targets = [(work, slice(GUARD + start, GUARD + start + 8))]
        for side in range(2):
            at_row = start - edge_starts[side]
            if 0 <= at_row < strip:
                targets.append((edge.at[side], slice(GUARD + at_row, GUARD + at_row + 8)))
        unpack(start, None, targets)

    first_lane = iota((8, LANES), 1) == 0
    end_lane = iota((8, LANES), 1) == LANES - 1

    def across(parts):
        up = [pltpu.roll(part, LANES - 1, axis=1) for part in parts] + [nothing]
        down = [nothing] + [pltpu.roll(part, 1, axis=1) for part in parts]
        return [
            jnp.where(end_lane, up[at + 1], up[at])
            - jnp.where(first_lane, down[at], down[at + 1])
            for at in range(lane_tiles)
        ]

    def advance(fields, flux, cross, first, last, shift):
        for start in range(first, last, 8):
            rows = slice(start, start + 8)
            fixed = slice(start + shift, start + shift + 8)
            after = slice(start + 1, start + 9)
            before = slice(start - 1, start + 7)
            slope_y = across([fields[0, at, rows, :] for at in range(lane_tiles)])
            flow = []
            for at in range(lane_tiles):
                wet = wwork[at, fixed, :]
                height = hwork[at, fixed, :]
                slope_x = fields[0, at, after, :] - fields[0, at, before, :]
                new_x = wet * (FRICTION * fields[1, at, rows, :] - PRESSURE * slope_x)
                new_y = wet * (FRICTION * fields[2, at, rows, :] - PRESSURE * slope_y[at])
                fields[1, at, rows, :] = new_x
                fields[2, at, rows, :] = new_y
                flux[at, rows, :] = height * new_x
                flow.append(height * new_y)
            for at, part in enumerate(across(flow)):
                cross[at, rows, :] = part
        for start in range(last - 8, first - 8, -8):
            rows = slice(start, start + 8)
            fixed = slice(start + shift, start + shift + 8)
            after = slice(start + 1, start + 9)
            before = slice(start - 1, start + 7)
            for at in range(lane_tiles):
                wet = wwork[at, fixed, :]
                level = fields[0, at, rows, :]
                energy = fields[3, at, rows, :]
                spill = (flux[at, after, :] - flux[at, before, :]) + cross[at, rows, :]
                fields[0, at, rows, :] = wet * (level - DIVERGE * spill + FORCING * energy)
                fields[3, at, rows, :] = wet * (
                    (1.0 - UPWIND - DAMPING) * energy + UPWIND * fields[3, at, before, :]
                )

    def inner_step(step, carry):
        advance(work, flux, cross, own_start, own_end, 0)
        return carry

    pl.semaphore_wait(barrier, others + 2)

    halos = []
    for way, (target, source_row, target_row, source_line, target_line) in enumerate(
        (
            (below, grid_rows - HALO, 0, own_table - TABLE_PAD, 0),
            (above, 0, HALO + grid_rows, 0, TABLE_PAD + own_table),
        )
    ):
        source_rows, target_rows = pl.ds(source_row, HALO), pl.ds(target_row, HALO)
        source_lines, target_lines = pl.ds(source_line, TABLE_PAD), pl.ds(target_line, TABLE_PAD)
        pairs = [
            (state_ref.at[0, :, source_rows], state_ext.at[:, target_rows]),
            (depth_ref.at[source_rows], depth_ext.at[target_rows]),
            (wet_ref.at[source_rows], wet_ext.at[target_rows]),
        ] + [(ref.at[source_lines], ext.at[target_lines]) for ref, ext in tables]
        for i, (source, destination) in enumerate(pairs):
            copy = pltpu.make_async_remote_copy(
                src_ref=source,
                dst_ref=destination,
                send_sem=halo_send.at[way, i],
                recv_sem=halo_recv.at[way, i],
                device_id={"tile": target},
                device_id_type=MESH,
            )
            copy.start()
            halos.append(copy)

    def send(which, peer, source, destination):
        pltpu.make_async_remote_copy(
            src_ref=source,
            dst_ref=destination,
            send_sem=group_send.at[which],
            recv_sem=group_recv.at[which],
            device_id={"member": peer},
            device_id_type=MESH,
        ).start()

    def to_group(which, source, destination):
        def one(step, carry):
            peer = lax.rem(me + step, members)
            send(which, peer, source(peer), destination)
            return carry

        lax.fori_loop(1, members, one, 0)

    def group_done(sems, which, ref, size):
        part = ref.at[pl.ds(0, size)]
        pltpu.make_async_copy(part, part, sems.at[which]).wait()

    to_group(0, lambda peer: lists.at[me], lists.at[me])
    lax.fori_loop(0, STEPS, inner_step, 0)

    slab = 2 * lane_tiles
    edge_owners = HALO // 4

    def build(field, first, last):
        for at in range(lane_tiles):
            slab_out[
                field, pl.ds(first * slab + at, 2 * (last - first), stride=lane_tiles), :
            ] = work[field, at, own_start + 2 * first : own_start + 2 * last, :]

    def slab_of(ref, fields, owner):
        return ref.at[
            pl.ds(fields[0], len(fields)), pl.ds(pl.multiple_of(owner * slab, slab), slab)
        ]

    def slabs_done(sems, which, ref, fields):
        part = ref.at[pl.ds(fields[0], len(fields)), pl.ds(0, others * slab)]
        pltpu.make_async_copy(part, part, sems.at[which]).wait()

    def send_slabs(chunk, first, last):
        count = last - first

        def one(step, carry):
            peer = first + lax.rem(me + step, count)

            @pl.when(peer != me)
            def _():
                fields = OUTWARD[chunk]
                send(2 + chunk, peer, slab_of(slab_out, fields, peer), slab_of(slab_in, fields, me))

            return carry

        lax.fori_loop(0, count, one, 0)

    if members > 2 * edge_owners:
        for field in range(4):
            build(field, edge_owners, members - edge_owners)
        send_slabs(0, edge_owners, members - edge_owners)

    for copy in halos:
        copy.wait_recv()
    for start in range(0, HALO, 8):
        unpack(start, tile > 0, [(edge.at[0], slice(GUARD + start, GUARD + start + 8))])
    for start in range(HALO + grid_rows, ext_rows, 8):
        at_row = start - edge_starts[1]
        unpack(
            start,
            tile < tiles - 1,
            [(edge.at[1], slice(GUARD + at_row, GUARD + at_row + 8))],
        )

    def edge_step(step, carry):
        for side in range(2):
            advance(
                edge.at[side],
                edge_flux.at[side],
                edge_cross.at[side],
                GUARD,
                GUARD + strip,
                edge_starts[side],
            )
        return carry

    lax.fori_loop(0, STEPS, edge_step, 0)
    for side in range(2):
        for start in (GUARD + 8, GUARD + 16):
            for field in range(4):
                for at in range(lane_tiles):
                    put = start + edge_starts[side]
                    work[field, at, put : put + 8, :] = edge[side, field, at, start : start + 8, :]

    first_line = TABLE_PAD - OBS_HALO // 2
    last_line = TABLE_PAD + own_table + OBS_HALO // 2
    offset = (cell_ext[...] & (SPACING - 1)).astype(BF16)
    place = iota((1, LANES), 1) & (SPACING - 1)
    chosen = [[], [], []]
    gathers = []
    for parity in range(2):
        for at in range(lane_tiles):
            owner = iota((LANES, LANES), 0) // SPACING + (parity * 64 + at * 16)
            gathers.append((owner == iota((LANES, LANES), 1)).astype(BF16))
            owner_t = iota((LANES, LANES), 1) // SPACING + (parity * 64 + at * 16)
            scatter = (owner_t == iota((LANES, LANES), 0)).astype(BF16)
            wanted = dot(offset, scatter).astype(jnp.int32) == place
            level = work[0, at, pl.ds(GUARD + parity, table_rows, stride=2), :]
            level = jnp.where(wanted, level, 0.0)
            for part, piece in zip(chosen, split3(level)):
                part.append(piece)
    gather = jnp.concatenate(gathers, axis=0)
    pieces = [dot(jnp.concatenate(part, axis=1), gather) for part in chosen]
    table[...] = ((pieces[2] + pieces[1]) + pieces[0]) * gain_ext[...]

    group_done(group_recv, 0, lists, others)
    base = obs_tile - TABLE_PAD * LANES
    for start in range(0, members, 4):
        slots = jnp.concatenate([lists[start + i] for i in range(4)], axis=0) - base
        found = lookup(
            table, first_line, last_line, slots // LANES, slots & (LANES - 1)
        )
        for i in range(4):
            pick_out[start + i] = found[2 * i : 2 * i + 2, :]
    pick_in[me] = pick_out[me]
    to_group(1, lambda peer: pick_out.at[peer], pick_in.at[me])

    for field in range(4):
        build(field, 0, edge_owners)
        build(field, members - edge_owners, members)
    send_slabs(0, 0, edge_owners)
    send_slabs(0, members - edge_owners, members)
    send_slabs(1, 0, members)
    own_slab = pl.ds(pl.multiple_of(me * slab, slab), slab)
    for field in range(4):
        slab_in[field, own_slab, :] = slab_out[field, own_slab, :]

    names = jnp.concatenate([own_list] * 4, axis=0)
    slots = names - base
    high, low = slots // LANES, slots & (LANES - 1)
    value = lookup(value_ext, first_line, last_line, high, low)
    error = lookup(error_ext, first_line, last_line, high, low)
    value, error = value[0:2], error[0:2]
    row_index = me * 2 + iota((2, LANES), 0)
    centre = obs_tile + row_index * 64
    dist = (own_list - centre).astype(F32) / radius
    counts = raw_count[...]
    slot = iota((1, LANES), 1) & 63
    limit = jnp.concatenate(
        [
            jnp.where(
                left_half, counts[0:1, 2 * i : 2 * i + 1], counts[0:1, 2 * i + 1 : 2 * i + 2]
            )
            for i in range(2)
        ],
        axis=0,
    )
    live = slot < limit
    precision = jnp.where(live, 1.0 / ((1.0 + 4.0 * dist * dist) * error), 0.0)

    size = 4 * members
    patch_of_line = iota((size, 2 * LANES), 0) // members
    patch_of_slot = iota((size, 2 * LANES), 1) // 64
    line, column = iota((size, size), 0) // members, iota((size, size), 1) // members
    same = line == column
    diagonal = iota((members, size), 0) == iota((members, size), 1) % members
    eye = jnp.where(diagonal, 1.0, 0.0)
    ones = jnp.where(same, 1.0, 0.0).astype(BF16)
    patch_ones = (iota((2 * LANES, size), 0) // 64 == iota((2 * LANES, size), 1) // members)
    patch_ones = jnp.where(patch_ones, 1.0, 0.0).astype(BF16)

    def blocks(packed):
        return jnp.where(same, jnp.concatenate([packed] * 4, axis=0), 0.0)

    group_done(group_recv, 1, pick_in, others)
    picked = jnp.concatenate([pick_in[:, i, :] for i in range(2)], axis=1)
    mean_eq = jnp.sum(picked, axis=0, keepdims=True) * (1.0 / members)
    spread = picked - mean_eq
    precision = jnp.concatenate([precision[0:1], precision[1:2]], axis=1)
    value = jnp.concatenate([value[0:1], value[1:2]], axis=1)
    weighted = spread * precision
    by_patch = jnp.where(
        patch_of_line == patch_of_slot, jnp.concatenate([spread] * 4, axis=0), 0.0
    )
    innovation = jnp.broadcast_to(precision * (value - mean_eq), weighted.shape)
    sums = lax.dot_general(
        jnp.concatenate([weighted, innovation], axis=0),
        by_patch,
        (((1,), (1,)), ((), ())),
        precision=HIGH,
        preferred_element_type=F32,
    )
    gram, proj = sums[:members], sums[members:]
    squares = exact_dot(weighted * spread, patch_ones)
    trace = jnp.sum(squares, axis=0, keepdims=True) + (members - 1.0) * members

    amat = gram + (members - 1.0) * eye

    def times(left, right):
        return dot6(left, blocks(right))

    def two_steps(square):
        second = times(square, square)
        third, fourth = times(second, square), times(second, second)
        after = 2.25 * square - 1.5 * second + 0.25 * third
        both = 2.25 * second - 1.5 * third + 0.25 * fourth
        return second, 2.25 * eye - 0.75 * (after + square) + 0.25 * both

    def three_steps(step, carry):
        square, inverse = carry
        second, factor = two_steps(square)
        once, twice = times(square, factor), times(second, factor)
        squared = times(factor, factor)
        product = 1.5 * factor - 0.5 * times(once, squared)
        moved = 1.5 * once - 0.5 * times(twice, squared)
        return times(moved, product), times(product, inverse)

    square, inverse = lax.fori_loop(0, (NS_ITERS - 2) // 3, three_steps, (amat / trace, eye))
    scale = (members - 1.0) ** 0.5 / jnp.sqrt(trace)
    early = times(proj, inverse)
    total = exact_dot(inverse, ones)
    _, factor = two_steps(square)
    early = times(early, factor)
    inverse = times(factor, inverse)
    total = times(factor, total)
    wbar = times(early, inverse) - times(early, total) * (1.0 / members)
    mix = scale * (inverse - total * (1.0 / members)) + wbar / trace + 1.0 / members
    mix = blocks(mix)
    mix_high, mix_low = split(mix)
    mix_both = jnp.concatenate([mix_high, mix_low], axis=0)

    for chunk, fields in enumerate(BACK):
        for field in fields:
            for coming, arriving in enumerate(OUTWARD):
                if field == arriving[0]:
                    slabs_done(group_recv, 2 + coming, slab_in, arriving)
            lines = [
                [
                    slab_in[field, pl.ds(row * lane_tiles + at, members, stride=slab), :]
                    for at in range(lane_tiles)
                ]
                for row in range(2)
            ]
            inputs = jnp.concatenate(
                [
                    jnp.concatenate(lines[row][2 * side : 2 * side + 2], axis=1)
                    for row in range(2)
                    for side in range(2)
                ],
                axis=0,
            )
            high, low = split(inputs)
            both = dot(mix_both, high)
            mixed = (both[size:] + dot(mix_high, low)) + both[:size]
            for row in range(2):
                for at in range(lane_tiles):
                    patch = row * 2 + at // 2
                    mix_out[
                        field, pl.ds(row * lane_tiles + at, members, stride=slab), :
                    ] = mixed[
                        patch * members : (patch + 1) * members,
                        (at % 2) * LANES : (at % 2 + 1) * LANES,
                    ]
            back_in[field, own_slab, :] = mix_out[field, own_slab, :]
        to_group(
            4 + chunk,
            lambda peer: slab_of(mix_out, fields, peer),
            slab_of(back_in, fields, me),
        )
    for chunk, fields in enumerate(BACK):
        slabs_done(group_recv, 4 + chunk, back_in, fields)
        for field in fields:
            for at in range(lane_tiles):
                out_ref[0, field, :, at * LANES : (at + 1) * LANES] = back_in[
                    field, pl.ds(at, grid_rows, stride=lane_tiles), :
                ]

    for copy in halos:
        copy.wait_send()
    group_done(group_send, 0, lists, others)
    group_done(group_send, 1, pick_out, others)
    for chunk, fields in enumerate(OUTWARD):
        slabs_done(group_send, 2 + chunk, slab_out, fields)
    for chunk, fields in enumerate(BACK):
        slabs_done(group_send, 4 + chunk, mix_out, fields)


def body(
    realization_array,
    water_depth,
    wet_mask,
    obs_cell,
    obs_value,
    obs_error,
    celer_gain,
    obs_list,
    obs_count,
):
    members = lax.axis_size("member")
    tiles = lax.axis_size("tile")
    grid_rows, width = water_depth.shape
    ext_rows = grid_rows + 2 * HALO
    lane_tiles = width // LANES
    own_table = obs_cell.shape[0] // LANES
    table_rows = own_table + 2 * TABLE_PAD
    slab_rows = members * 2 * lane_tiles
    strip = 2 * HALO + 2 * GUARD
    deep = ext_rows + 2 * GUARD
    as_lines = lambda array: array.reshape(own_table, LANES)
    far = pl.BlockSpec(memory_space=pltpu.HBM)
    near = pl.BlockSpec(memory_space=pltpu.VMEM)
    return pl.pallas_call(
        functools.partial(kernel, members, tiles, grid_rows),
        out_shape=jax.ShapeDtypeStruct(realization_array.shape, F32),
        in_specs=[far] * 9,
        out_specs=near,
        scratch_shapes=[
            pltpu.VMEM((4, ext_rows, width), F32),
            pltpu.VMEM((ext_rows, width), F32),
            pltpu.VMEM((ext_rows, width), jnp.int32),
            pltpu.VMEM((table_rows, LANES), jnp.int32),
            pltpu.VMEM((table_rows, LANES), F32),
            pltpu.VMEM((table_rows, LANES), F32),
            pltpu.VMEM((table_rows, LANES), F32),
            pltpu.VMEM((4, lane_tiles, deep, LANES), F32),
            pltpu.VMEM((2, 4, lane_tiles, strip, LANES), F32),
            pltpu.VMEM((lane_tiles, deep, LANES), F32),
            pltpu.VMEM((lane_tiles, deep, LANES), F32),
            pltpu.VMEM((lane_tiles, deep, LANES), F32),
            pltpu.VMEM((lane_tiles, deep, LANES), F32),
            pltpu.VMEM((2, lane_tiles, strip, LANES), F32),
            pltpu.VMEM((2, lane_tiles, strip, LANES), F32),
            pltpu.VMEM(obs_list.shape[1:], jnp.int32),
            pltpu.VMEM(obs_count.shape, jnp.int32),
            pltpu.VMEM((8, LANES), jnp.int32),
            pltpu.VMEM((members, 2, LANES), jnp.int32),
            pltpu.VMEM((table_rows, LANES), F32),
            pltpu.VMEM((members, 2, LANES), F32),
            pltpu.VMEM((members, 2, LANES), F32),
            pltpu.VMEM((4, slab_rows, LANES), F32),
            pltpu.VMEM((4, slab_rows, LANES), F32),
            pltpu.VMEM((4, slab_rows, LANES), F32),
            pltpu.VMEM((4, slab_rows, LANES), F32),
            pltpu.SemaphoreType.DMA((9,)),
            pltpu.SemaphoreType.DMA((2, 7)),
            pltpu.SemaphoreType.DMA((2, 7)),
            pltpu.SemaphoreType.DMA((4 + len(BACK),)),
            pltpu.SemaphoreType.DMA((4 + len(BACK),)),
        ],
        compiler_params=pltpu.CompilerParams(
            collective_id=0, has_side_effects=True, vmem_limit_bytes=32 * 1024 * 1024
        ),
    )(
        *[
            pltpu.with_memory_space_constraint(array, pltpu.HBM)
            for array in (
                realization_array,
                water_depth,
                wet_mask,
                as_lines(obs_cell),
                as_lines(celer_gain),
                as_lines(obs_value),
                as_lines(obs_error),
                obs_list,
                obs_count,
            )
        ]
    )


def solution(mesh):
    return jax.shard_map(
        body,
        mesh=mesh,
        in_specs=(
            P("member", None, "tile", None),
            P("tile", None),
            P("tile", None),
            P("tile"),
            P("tile"),
            P("tile"),
            P("tile"),
            P("tile", "member", None),
            P("tile", "member"),
        ),
        out_specs=P("member", None, "tile", None),
        check_vma=False,
    )
```

```python
import functools

import jax
import jax.numpy as jnp
from jax import lax
from jax.experimental import pallas as pl
from jax.experimental.pallas import tpu as pltpu
from jax.sharding import PartitionSpec as P

MESH = pl.DeviceIdType.MESH
HIGH = lax.Precision.HIGHEST
F32 = jnp.float32
BF16 = jnp.bfloat16

REGION_POINTS = 256
OUTWARD = ((0, 1), (2, 3))
BACK = ((0,), (1,), (2, 3))
STEPS = 4
NS_ITERS = 14
SPACING = 8

FRICTION = 0.98
PRESSURE = 0.25
DIVERGE = 0.25
FORCING = 0.05
UPWIND = 0.4
DAMPING = 0.02

LANES = 128
GUARD = 8
HALO = 16
OBS_HALO = 8
TABLE_PAD = 8


def iota(shape, dim):
    return lax.broadcasted_iota(jnp.int32, shape, dim)


def dot(left, right, precision=None):
    return lax.dot_general(
        left, right, (((1,), (0,)), ((), ())), precision=precision, preferred_element_type=F32
    )


def split(x):
    high = x.astype(BF16)
    return high, (x - high.astype(F32)).astype(BF16)


def split3(x):
    high, _ = split(x)
    middle, low = split(x - high.astype(F32))
    return high, middle, low


def dot6(left, right):
    left_high, left_middle, left_low = split3(left)
    right_high, right_middle, right_low = split3(right)
    rows = left.shape[0]
    straight = jnp.concatenate([left_high, left_middle], axis=1)
    crossed = jnp.concatenate([left_middle, left_high], axis=1)
    large = dot(
        jnp.concatenate([straight, crossed], axis=0),
        jnp.concatenate([right_high, right_middle], axis=0),
    )
    small = dot(
        jnp.concatenate([left_low, left_high], axis=1),
        jnp.concatenate([right_high, right_low], axis=0),
    )
    return (small + large[rows:]) + large[:rows]


def exact_dot(left, ones):
    rows = left.shape[0]
    parts = dot(jnp.concatenate(split3(left), axis=0), ones)
    return (parts[2 * rows :] + parts[rows : 2 * rows]) + parts[:rows]


def lookup(table, first, last, high, low):
    found = jnp.zeros(high.shape, table.dtype)
    for row in range(first, last):
        line = jnp.broadcast_to(table[row : row + 1, :], high.shape)
        found = jnp.where(
            high == row,
            jnp.take_along_axis(line, low, axis=1, mode="promise_in_bounds"),
            found,
        )
    return found


def kernel(
    members,
    tiles,
    grid_rows,
    state_ref,
    depth_ref,
    wet_ref,
    cell_ref,
    gain_ref,
    value_ref,
    error_ref,
    list_ref,
    count_ref,
    out_ref,
    state_ext,
    depth_ext,
    wet_ext,
    cell_ext,
    gain_ext,
    value_ext,
    error_ext,
    work,
    edge,
    hwork,
    wwork,
    flux,
    cross,
    edge_flux,
    edge_cross,
    raw_list,
    raw_count,
    pack,
    lists,
    table,
    pick_out,
    pick_in,
    slab_out,
    slab_in,
    mix_out,
    back_in,
    local_sem,
    halo_send,
    halo_recv,
    group_send,
    group_recv,
):
    me = lax.axis_index("member")
    tile = lax.axis_index("tile")
    above = lax.rem(tile + tiles - 1, tiles)
    below = lax.rem(tile + 1, tiles)
    ext_rows = grid_rows + 2 * HALO
    lane_tiles = 4
    obs_tile = grid_rows * 64
    radius = obs_tile // 8
    own_table = obs_tile // LANES
    table_rows = own_table + 2 * TABLE_PAD
    others = members - 1

    barrier = pltpu.get_barrier_semaphore()

    def greet(step, carry):
        peer = lax.rem(me + step, members)
        pl.semaphore_signal(barrier, inc=1, device_id={"member": peer}, device_id_type=MESH)
        return carry

    pl.semaphore_signal(barrier, inc=1, device_id={"tile": above}, device_id_type=MESH)
    pl.semaphore_signal(barrier, inc=1, device_id={"tile": below}, device_id_type=MESH)
    lax.fori_loop(1, members, greet, 0)

    own_rows = pl.ds(HALO, grid_rows)
    own_lines = pl.ds(TABLE_PAD, own_table)
    tables = (
        (cell_ref, cell_ext),
        (gain_ref, gain_ext),
        (value_ref, value_ext),
        (error_ref, error_ext),
    )
    pairs = [
        (list_ref.at[0], raw_list),
        (count_ref, raw_count),
        (state_ref.at[0], state_ext.at[:, own_rows]),
        (depth_ref, depth_ext.at[own_rows]),
        (wet_ref, wet_ext.at[own_rows]),
    ] + [(ref, ext.at[own_lines]) for ref, ext in tables]
    local = [
        pltpu.make_async_copy(source, destination, local_sem.at[i])
        for i, (source, destination) in enumerate(pairs)
    ]
    for copy in local:
        copy.start()

    nothing = jnp.zeros((8, LANES), F32)
    strip = 2 * HALO
    own_start = GUARD + HALO
    own_end = own_start + grid_rows
    for at in range(lane_tiles):
        for field in (0, 3):
            work[field, at, own_start - 8 : own_start, :] = nothing
            work[field, at, own_end : own_end + 8, :] = nothing
            for side in range(2):
                edge[side, field, at, 0:GUARD, :] = nothing
                edge[side, field, at, GUARD + strip :, :] = nothing
        flux[at, own_start - 8 : own_start, :] = nothing
        flux[at, own_end : own_end + 8, :] = nothing
        for side in range(2):
            edge_flux[side, at, 0:GUARD, :] = nothing
            edge_flux[side, at, GUARD + strip :, :] = nothing
    pack[...] = jnp.zeros(pack.shape, jnp.int32)

    local[0].wait()
    pack[0:4, 0:64] = raw_list[...]
    packed = pack[...]
    turned = pltpu.roll(packed, 64, axis=1)
    left_half = iota((1, LANES), 1) < 64
    own_list = jnp.concatenate(
        [
            jnp.where(left_half, packed[0:1], turned[1:2]),
            jnp.where(left_half, packed[2:3], turned[3:4]),
        ],
        axis=0,
    )
    lists[me] = own_list
    for copy in local[1:]:
        copy.wait()

    def unpack(start, inside, targets):
        rows = slice(start, start + 8)
        put = slice(GUARD + start, GUARD + start + 8)
        for at in range(lane_tiles):
            lanes = slice(at * LANES, (at + 1) * LANES)
            parts = [state_ext[field, rows, lanes] for field in range(4)]
            if inside is not None:
                parts = [jnp.where(inside, part, 0.0) for part in parts]
            for target, target_rows in targets:
                for field in range(4):
                    target[field, at, target_rows, :] = parts[field]
            wet = wet_ext[rows, lanes].astype(F32)
            if inside is not None:
                wet = jnp.where(inside, wet, 0.0)
            wwork[at, put, :] = wet
            hwork[at, put, :] = depth_ext[rows, lanes]

    edge_starts = (0, ext_rows - strip)
    for start in range(HALO, HALO + grid_rows, 8):
        targets = [(work, slice(GUARD + start, GUARD + start + 8))]
        for side in range(2):
            at_row = start - edge_starts[side]
            if 0 <= at_row < strip:
                targets.append((edge.at[side], slice(GUARD + at_row, GUARD + at_row + 8)))
        unpack(start, None, targets)

    first_lane = iota((8, LANES), 1) == 0
    end_lane = iota((8, LANES), 1) == LANES - 1

    def across(parts):
        up = [pltpu.roll(part, LANES - 1, axis=1) for part in parts] + [nothing]
        down = [nothing] + [pltpu.roll(part, 1, axis=1) for part in parts]
        return [
            jnp.where(end_lane, up[at + 1], up[at])
            - jnp.where(first_lane, down[at], down[at + 1])
            for at in range(lane_tiles)
        ]

    def advance(fields, flux, cross, first, last, shift, margin=0):
        for start in range(first, last, 8):
            rows = slice(start, start + 8)
            fixed = slice(start + shift, start + shift + 8)
            after = slice(start + 1, start + 9)
            before = slice(start - 1, start + 7)
            whole = first + margin <= start < last - margin
            if whole:
                slope_y = across([fields[0, at, rows, :] for at in range(lane_tiles)])
            flow = []
            for at in range(lane_tiles):
                wet = wwork[at, fixed, :]
                height = hwork[at, fixed, :]
                slope_x = fields[0, at, after, :] - fields[0, at, before, :]
                new_x = wet * (FRICTION * fields[1, at, rows, :] - PRESSURE * slope_x)
                flux[at, rows, :] = height * new_x
                if not whole:
                    continue
                new_y = wet * (FRICTION * fields[2, at, rows, :] - PRESSURE * slope_y[at])
                fields[1, at, rows, :] = new_x
                fields[2, at, rows, :] = new_y
                flow.append(height * new_y)
            if whole:
                for at, part in enumerate(across(flow)):
                    cross[at, rows, :] = part
        for start in range(last - margin - 8, first + margin - 8, -8):
            rows = slice(start, start + 8)
            fixed = slice(start + shift, start + shift + 8)
            after = slice(start + 1, start + 9)
            before = slice(start - 1, start + 7)
            for at in range(lane_tiles):
                wet = wwork[at, fixed, :]
                level = fields[0, at, rows, :]
                energy = fields[3, at, rows, :]
                spill = (flux[at, after, :] - flux[at, before, :]) + cross[at, rows, :]
                fields[0, at, rows, :] = wet * (level - DIVERGE * spill + FORCING * energy)
                fields[3, at, rows, :] = wet * (
                    (1.0 - UPWIND - DAMPING) * energy + UPWIND * fields[3, at, before, :]
                )

    def inner_step(step, carry):
        advance(work, flux, cross, own_start, own_end, 0)
        return carry

    pl.semaphore_wait(barrier, others + 2)

    halos = []
    for way, (target, source_row, target_row, source_line, target_line) in enumerate(
        (
            (below, grid_rows - HALO, 0, own_table - TABLE_PAD, 0),
            (above, 0, HALO + grid_rows, 0, TABLE_PAD + own_table),
        )
    ):
        source_rows, target_rows = pl.ds(source_row, HALO), pl.ds(target_row, HALO)
        source_lines, target_lines = pl.ds(source_line, TABLE_PAD), pl.ds(target_line, TABLE_PAD)
        pairs = [
            (state_ref.at[0, :, source_rows], state_ext.at[:, target_rows]),
            (depth_ref.at[source_rows], depth_ext.at[target_rows]),
            (wet_ref.at[source_rows], wet_ext.at[target_rows]),
        ] + [(ref.at[source_lines], ext.at[target_lines]) for ref, ext in tables]
        for i, (source, destination) in enumerate(pairs):
            copy = pltpu.make_async_remote_copy(
                src_ref=source,
                dst_ref=destination,
                send_sem=halo_send.at[way, i],
                recv_sem=halo_recv.at[way, i],
                device_id={"tile": target},
                device_id_type=MESH,
            )
            halos.append(copy)

    for i in range(7):
        for way in range(2):
            halos[way * 7 + i].start()

    def send(which, peer, source, destination):
        pltpu.make_async_remote_copy(
            src_ref=source,
            dst_ref=destination,
            send_sem=group_send.at[which],
            recv_sem=group_recv.at[which],
            device_id={"member": peer},
            device_id_type=MESH,
        ).start()

    def to_group(which, source, destination):
        def one(step, carry):
            peer = lax.rem(me + step, members)
            send(which, peer, source(peer), destination)
            return carry

        lax.fori_loop(1, members, one, 0)

    def group_done(sems, which, ref, size):
        part = ref.at[pl.ds(0, size)]
        pltpu.make_async_copy(part, part, sems.at[which]).wait()

    to_group(0, lambda peer: lists.at[me], lists.at[me])
    lax.fori_loop(0, STEPS, inner_step, 0)

    slab = 2 * lane_tiles
    edge_owners = HALO // 4

    def build(field, first, last):
        for at in range(lane_tiles):
            slab_out[
                field, pl.ds(first * slab + at, 2 * (last - first), stride=lane_tiles), :
            ] = work[field, at, own_start + 2 * first : own_start + 2 * last, :]

    def slab_of(ref, fields, owner):
        return ref.at[
            pl.ds(fields[0], len(fields)), pl.ds(pl.multiple_of(owner * slab, slab), slab)
        ]

    def slabs_done(sems, which, ref, fields):
        part = ref.at[pl.ds(fields[0], len(fields)), pl.ds(0, others * slab)]
        pltpu.make_async_copy(part, part, sems.at[which]).wait()

    def send_slabs(chunk, first, last):
        count = last - first

        def one(step, carry):
            peer = first + lax.rem(me + step, count)

            @pl.when(peer != me)
            def _():
                fields = OUTWARD[chunk]
                send(2 + chunk, peer, slab_of(slab_out, fields, peer), slab_of(slab_in, fields, me))

            return carry

        lax.fori_loop(0, count, one, 0)

    if members > 2 * edge_owners:
        for field in range(4):
            build(field, edge_owners, members - edge_owners)
        send_slabs(0, edge_owners, members - edge_owners)

    for copy in halos:
        copy.wait_recv()
    for start in range(0, HALO, 8):
        unpack(start, tile > 0, [(edge.at[0], slice(GUARD + start, GUARD + start + 8))])
    for start in range(HALO + grid_rows, ext_rows, 8):
        at_row = start - edge_starts[1]
        unpack(
            start,
            tile < tiles - 1,
            [(edge.at[1], slice(GUARD + at_row, GUARD + at_row + 8))],
        )

    def edge_step(margin):
        for side in range(2):
            advance(
                edge.at[side],
                edge_flux.at[side],
                edge_cross.at[side],
                GUARD,
                GUARD + strip,
                edge_starts[side],
                margin,
            )

    def outer_step(step, carry):
        edge_step(0)
        return carry

    lax.fori_loop(0, STEPS - 1, outer_step, 0)
    edge_step(8)

    def from_edges(field):
        for side in range(2):
            for start in (GUARD + 8, GUARD + 16):
                for at in range(lane_tiles):
                    put = start + edge_starts[side]
                    work[field, at, put : put + 8, :] = edge[side, field, at, start : start + 8, :]

    from_edges(0)

    first_line = TABLE_PAD - OBS_HALO // 2
    last_line = TABLE_PAD + own_table + OBS_HALO // 2
    offset = (cell_ext[...] & (SPACING - 1)).astype(BF16)
    place = iota((1, LANES), 1) & (SPACING - 1)
    chosen = [[], [], []]
    gathers = []
    for parity in range(2):
        for at in range(lane_tiles):
            owner = iota((LANES, LANES), 0) // SPACING + (parity * 64 + at * 16)
            gathers.append((owner == iota((LANES, LANES), 1)).astype(BF16))
            owner_t = iota((LANES, LANES), 1) // SPACING + (parity * 64 + at * 16)
            scatter = (owner_t == iota((LANES, LANES), 0)).astype(BF16)
            wanted = dot(offset, scatter).astype(jnp.int32) == place
            level = work[0, at, pl.ds(GUARD + parity, table_rows, stride=2), :]
            level = jnp.where(wanted, level, 0.0)
            for part, piece in zip(chosen, split3(level)):
                part.append(piece)
    gather = jnp.concatenate(gathers, axis=0)
    pieces = [dot(jnp.concatenate(part, axis=1), gather) for part in chosen]
    table[...] = ((pieces[2] + pieces[1]) + pieces[0]) * gain_ext[...]

    group_done(group_recv, 0, lists, others)
    base = obs_tile - TABLE_PAD * LANES
    for start in range(0, members, 4):
        slots = jnp.concatenate([lists[start + i] for i in range(4)], axis=0) - base
        found = lookup(
            table, first_line, last_line, slots // LANES, slots & (LANES - 1)
        )
        for i in range(4):
            pick_out[start + i] = found[2 * i : 2 * i + 2, :]
    pick_in[me] = pick_out[me]
    to_group(1, lambda peer: pick_out.at[peer], pick_in.at[me])

    for field in range(1, 4):
        from_edges(field)
    for field in range(4):
        build(field, 0, edge_owners)
        build(field, members - edge_owners, members)
    send_slabs(0, 0, edge_owners)
    send_slabs(0, members - edge_owners, members)
    send_slabs(1, 0, members)
    own_slab = pl.ds(pl.multiple_of(me * slab, slab), slab)
    for field in range(4):
        slab_in[field, own_slab, :] = slab_out[field, own_slab, :]

    names = jnp.concatenate([own_list] * 4, axis=0)
    slots = names - base
    high, low = slots // LANES, slots & (LANES - 1)
    value = lookup(value_ext, first_line, last_line, high, low)
    error = lookup(error_ext, first_line, last_line, high, low)
    value, error = value[0:2], error[0:2]
    row_index = me * 2 + iota((2, LANES), 0)
    centre = obs_tile + row_index * 64
    dist = (own_list - centre).astype(F32) / radius
    counts = raw_count[...]
    slot = iota((1, LANES), 1) & 63
    limit = jnp.concatenate(
        [
            jnp.where(
                left_half, counts[0:1, 2 * i : 2 * i + 1], counts[0:1, 2 * i + 1 : 2 * i + 2]
            )
            for i in range(2)
        ],
        axis=0,
    )
    live = slot < limit
    precision = jnp.where(live, 1.0 / ((1.0 + 4.0 * dist * dist) * error), 0.0)

    size = 4 * members
    patch_of_line = iota((size, 2 * LANES), 0) // members
    patch_of_slot = iota((size, 2 * LANES), 1) // 64
    line, column = iota((size, size), 0) // members, iota((size, size), 1) // members
    same = line == column
    diagonal = iota((members, size), 0) == iota((members, size), 1) % members
    eye = jnp.where(diagonal, 1.0, 0.0)
    ones = jnp.where(same, 1.0, 0.0).astype(BF16)
    patch_ones = (iota((2 * LANES, size), 0) // 64 == iota((2 * LANES, size), 1) // members)
    patch_ones = jnp.where(patch_ones, 1.0, 0.0).astype(BF16)

    def blocks(packed):
        return jnp.where(same, jnp.concatenate([packed] * 4, axis=0), 0.0)

    group_done(group_recv, 1, pick_in, others)
    picked = jnp.concatenate([pick_in[:, i, :] for i in range(2)], axis=1)
    mean_eq = jnp.sum(picked, axis=0, keepdims=True) * (1.0 / members)
    spread = picked - mean_eq
    precision = jnp.concatenate([precision[0:1], precision[1:2]], axis=1)
    value = jnp.concatenate([value[0:1], value[1:2]], axis=1)
    weighted = spread * precision
    by_patch = jnp.where(
        patch_of_line == patch_of_slot, jnp.concatenate([spread] * 4, axis=0), 0.0
    )
    innovation = jnp.broadcast_to(precision * (value - mean_eq), weighted.shape)
    sums = lax.dot_general(
        jnp.concatenate([weighted, innovation], axis=0),
        by_patch,
        (((1,), (1,)), ((), ())),
        precision=HIGH,
        preferred_element_type=F32,
    )
    gram, proj = sums[:members], sums[members:]
    squares = exact_dot(weighted * spread, patch_ones)
    trace = jnp.sum(squares, axis=0, keepdims=True) + (members - 1.0) * members

    amat = gram + (members - 1.0) * eye

    def times(left, right):
        return dot6(left, blocks(right))

    def two_steps(square):
        second = times(square, square)
        third, fourth = times(second, square), times(second, second)
        after = 2.25 * square - 1.5 * second + 0.25 * third
        both = 2.25 * second - 1.5 * third + 0.25 * fourth
        return second, 2.25 * eye - 0.75 * (after + square) + 0.25 * both

    def three_steps(step, carry):
        square, inverse = carry
        second, factor = two_steps(square)
        once, twice = times(square, factor), times(second, factor)
        squared = times(factor, factor)
        product = 1.5 * factor - 0.5 * times(once, squared)
        moved = 1.5 * once - 0.5 * times(twice, squared)
        return times(moved, product), times(product, inverse)

    square, inverse = lax.fori_loop(0, (NS_ITERS - 2) // 3, three_steps, (amat / trace, eye))
    scale = (members - 1.0) ** 0.5 / jnp.sqrt(trace)
    early = times(proj, inverse)
    total = exact_dot(inverse, ones)
    _, factor = two_steps(square)
    early = times(early, factor)
    inverse = times(factor, inverse)
    total = times(factor, total)
    wbar = times(early, inverse) - times(early, total) * (1.0 / members)
    mix = scale * (inverse - total * (1.0 / members)) + wbar / trace + 1.0 / members
    mix = blocks(mix)
    mix_high, mix_low = split(mix)
    mix_both = jnp.concatenate([mix_high, mix_low], axis=0)

    for chunk, fields in enumerate(BACK):
        for field in fields:
            for coming, arriving in enumerate(OUTWARD):
                if field == arriving[0]:
                    slabs_done(group_recv, 2 + coming, slab_in, arriving)
            lines = [
                [
                    slab_in[field, pl.ds(row * lane_tiles + at, members, stride=slab), :]
                    for at in range(lane_tiles)
                ]
                for row in range(2)
            ]
            inputs = jnp.concatenate(
                [
                    jnp.concatenate(lines[row][2 * side : 2 * side + 2], axis=1)
                    for row in range(2)
                    for side in range(2)
                ],
                axis=0,
            )
            high, low = split(inputs)
            both = dot(mix_both, high)
            mixed = (both[size:] + dot(mix_high, low)) + both[:size]
            for row in range(2):
                for at in range(lane_tiles):
                    patch = row * 2 + at // 2
                    mix_out[
                        field, pl.ds(row * lane_tiles + at, members, stride=slab), :
                    ] = mixed[
                        patch * members : (patch + 1) * members,
                        (at % 2) * LANES : (at % 2 + 1) * LANES,
                    ]
            back_in[field, own_slab, :] = mix_out[field, own_slab, :]
        to_group(
            4 + chunk,
            lambda peer: slab_of(mix_out, fields, peer),
            slab_of(back_in, fields, me),
        )
    for chunk, fields in enumerate(BACK):
        slabs_done(group_recv, 4 + chunk, back_in, fields)
        for field in fields:
            for at in range(lane_tiles):
                out_ref[0, field, :, at * LANES : (at + 1) * LANES] = back_in[
                    field, pl.ds(at, grid_rows, stride=lane_tiles), :
                ]

    for copy in halos:
        copy.wait_send()
    group_done(group_send, 0, lists, others)
    group_done(group_send, 1, pick_out, others)
    for chunk, fields in enumerate(OUTWARD):
        slabs_done(group_send, 2 + chunk, slab_out, fields)
    for chunk, fields in enumerate(BACK):
        slabs_done(group_send, 4 + chunk, mix_out, fields)


def body(
    realization_array,
    water_depth,
    wet_mask,
    obs_cell,
    obs_value,
    obs_error,
    celer_gain,
    obs_list,
    obs_count,
):
    members = lax.axis_size("member")
    tiles = lax.axis_size("tile")
    grid_rows, width = water_depth.shape
    ext_rows = grid_rows + 2 * HALO
    lane_tiles = width // LANES
    own_table = obs_cell.shape[0] // LANES
    table_rows = own_table + 2 * TABLE_PAD
    slab_rows = members * 2 * lane_tiles
    strip = 2 * HALO + 2 * GUARD
    deep = ext_rows + 2 * GUARD
    as_lines = lambda array: array.reshape(own_table, LANES)
    far = pl.BlockSpec(memory_space=pltpu.HBM)
    near = pl.BlockSpec(memory_space=pltpu.VMEM)
    return pl.pallas_call(
        functools.partial(kernel, members, tiles, grid_rows),
        out_shape=jax.ShapeDtypeStruct(realization_array.shape, F32),
        in_specs=[far] * 9,
        out_specs=near,
        scratch_shapes=[
            pltpu.VMEM((4, ext_rows, width), F32),
            pltpu.VMEM((ext_rows, width), F32),
            pltpu.VMEM((ext_rows, width), jnp.int32),
            pltpu.VMEM((table_rows, LANES), jnp.int32),
            pltpu.VMEM((table_rows, LANES), F32),
            pltpu.VMEM((table_rows, LANES), F32),
            pltpu.VMEM((table_rows, LANES), F32),
            pltpu.VMEM((4, lane_tiles, deep, LANES), F32),
            pltpu.VMEM((2, 4, lane_tiles, strip, LANES), F32),
            pltpu.VMEM((lane_tiles, deep, LANES), F32),
            pltpu.VMEM((lane_tiles, deep, LANES), F32),
            pltpu.VMEM((lane_tiles, deep, LANES), F32),
            pltpu.VMEM((lane_tiles, deep, LANES), F32),
            pltpu.VMEM((2, lane_tiles, strip, LANES), F32),
            pltpu.VMEM((2, lane_tiles, strip, LANES), F32),
            pltpu.VMEM(obs_list.shape[1:], jnp.int32),
            pltpu.VMEM(obs_count.shape, jnp.int32),
            pltpu.VMEM((8, LANES), jnp.int32),
            pltpu.VMEM((members, 2, LANES), jnp.int32),
            pltpu.VMEM((table_rows, LANES), F32),
            pltpu.VMEM((members, 2, LANES), F32),
            pltpu.VMEM((members, 2, LANES), F32),
            pltpu.VMEM((4, slab_rows, LANES), F32),
            pltpu.VMEM((4, slab_rows, LANES), F32),
            pltpu.VMEM((4, slab_rows, LANES), F32),
            pltpu.VMEM((4, slab_rows, LANES), F32),
            pltpu.SemaphoreType.DMA((9,)),
            pltpu.SemaphoreType.DMA((2, 7)),
            pltpu.SemaphoreType.DMA((2, 7)),
            pltpu.SemaphoreType.DMA((4 + len(BACK),)),
            pltpu.SemaphoreType.DMA((4 + len(BACK),)),
        ],
        compiler_params=pltpu.CompilerParams(
            collective_id=0, has_side_effects=True, vmem_limit_bytes=32 * 1024 * 1024
        ),
    )(
        *[
            pltpu.with_memory_space_constraint(array, pltpu.HBM)
            for array in (
                realization_array,
                water_depth,
                wet_mask,
                as_lines(obs_cell),
                as_lines(celer_gain),
                as_lines(obs_value),
                as_lines(obs_error),
                obs_list,
                obs_count,
            )
        ]
    )


def solution(mesh):
    return jax.shard_map(
        body,
        mesh=mesh,
        in_specs=(
            P("member", None, "tile", None),
            P("tile", None),
            P("tile", None),
            P("tile"),
            P("tile"),
            P("tile"),
            P("tile"),
            P("tile", "member", None),
            P("tile", "member"),
        ),
        out_specs=P("member", None, "tile", None),
        check_vma=False,
    )
```

```python
import functools

import jax
import jax.numpy as jnp
from jax import lax
from jax.experimental import pallas as pl
from jax.experimental.pallas import tpu as pltpu
from jax.sharding import PartitionSpec as P

MESH = pl.DeviceIdType.MESH
HIGH = lax.Precision.HIGHEST
F32 = jnp.float32
BF16 = jnp.bfloat16

REGION_POINTS = 256
OUTWARD = ((0, 1), (2, 3))
BACK = ((0,), (1,), (2, 3))
STEPS = 4
NS_ITERS = 14
SPACING = 8

FRICTION = 0.98
PRESSURE = 0.25
DIVERGE = 0.25
FORCING = 0.05
UPWIND = 0.4
DAMPING = 0.02

LANES = 128
GUARD = 8
HALO = 16
OBS_HALO = 8
TABLE_PAD = 8


def iota(shape, dim):
    return lax.broadcasted_iota(jnp.int32, shape, dim)


def dot(left, right, precision=None):
    return lax.dot_general(
        left, right, (((1,), (0,)), ((), ())), precision=precision, preferred_element_type=F32
    )


def split(x):
    high = x.astype(BF16)
    return high, (x - high.astype(F32)).astype(BF16)


def split3(x):
    high, _ = split(x)
    middle, low = split(x - high.astype(F32))
    return high, middle, low


def dot6(left, right):
    left_high, left_middle, left_low = split3(left)
    right_high, right_middle, right_low = split3(right)
    rows = left.shape[0]
    straight = jnp.concatenate([left_high, left_middle], axis=1)
    crossed = jnp.concatenate([left_middle, left_high], axis=1)
    large = dot(
        jnp.concatenate([straight, crossed], axis=0),
        jnp.concatenate([right_high, right_middle], axis=0),
    )
    small = dot(
        jnp.concatenate([left_low, left_high], axis=1),
        jnp.concatenate([right_high, right_low], axis=0),
    )
    return (small + large[rows:]) + large[:rows]


def exact_dot(left, ones):
    rows = left.shape[0]
    parts = dot(jnp.concatenate(split3(left), axis=0), ones)
    return (parts[2 * rows :] + parts[rows : 2 * rows]) + parts[:rows]


def lookup(table, first, last, high, low):
    found = jnp.zeros(high.shape, table.dtype)
    for row in range(first, last):
        line = jnp.broadcast_to(table[row : row + 1, :], high.shape)
        found = jnp.where(
            high == row,
            jnp.take_along_axis(line, low, axis=1, mode="promise_in_bounds"),
            found,
        )
    return found


def kernel(
    members,
    tiles,
    grid_rows,
    state_ref,
    depth_ref,
    wet_ref,
    cell_ref,
    gain_ref,
    value_ref,
    error_ref,
    list_ref,
    count_ref,
    out_ref,
    state_ext,
    depth_ext,
    wet_ext,
    cell_ext,
    gain_ext,
    value_ext,
    error_ext,
    work,
    edge,
    hwork,
    wwork,
    flux,
    cross,
    edge_flux,
    edge_cross,
    raw_list,
    raw_count,
    pack,
    lists,
    table,
    pick_out,
    pick_in,
    slab_out,
    slab_in,
    mix_out,
    back_in,
    local_sem,
    halo_send,
    halo_recv,
    group_send,
    group_recv,
):
    me = lax.axis_index("member")
    tile = lax.axis_index("tile")
    above = lax.rem(tile + tiles - 1, tiles)
    below = lax.rem(tile + 1, tiles)
    ext_rows = grid_rows + 2 * HALO
    lane_tiles = 4
    obs_tile = grid_rows * 64
    radius = obs_tile // 8
    own_table = obs_tile // LANES
    table_rows = own_table + 2 * TABLE_PAD
    others = members - 1

    barrier = pltpu.get_barrier_semaphore()

    def greet(step, carry):
        peer = lax.rem(me + step, members)
        pl.semaphore_signal(barrier, inc=1, device_id={"member": peer}, device_id_type=MESH)
        return carry

    pl.semaphore_signal(barrier, inc=1, device_id={"tile": above}, device_id_type=MESH)
    pl.semaphore_signal(barrier, inc=1, device_id={"tile": below}, device_id_type=MESH)
    lax.fori_loop(1, members, greet, 0)

    own_rows = pl.ds(HALO, grid_rows)
    own_lines = pl.ds(TABLE_PAD, own_table)
    tables = (
        (cell_ref, cell_ext),
        (gain_ref, gain_ext),
        (value_ref, value_ext),
        (error_ref, error_ext),
    )
    pairs = [
        (list_ref.at[0], raw_list),
        (count_ref, raw_count),
        (state_ref.at[0], state_ext.at[:, own_rows]),
        (depth_ref, depth_ext.at[own_rows]),
        (wet_ref, wet_ext.at[own_rows]),
    ] + [(ref, ext.at[own_lines]) for ref, ext in tables]
    local = [
        pltpu.make_async_copy(source, destination, local_sem.at[i])
        for i, (source, destination) in enumerate(pairs)
    ]
    for copy in local:
        copy.start()

    nothing = jnp.zeros((8, LANES), F32)
    strip = 2 * HALO
    own_start = GUARD + HALO
    own_end = own_start + grid_rows
    for at in range(lane_tiles):
        for field in (0, 3):
            work[field, at, own_start - 8 : own_start, :] = nothing
            work[field, at, own_end : own_end + 8, :] = nothing
            for side in range(2):
                edge[side, field, at, 0:GUARD, :] = nothing
                edge[side, field, at, GUARD + strip :, :] = nothing
        flux[at, own_start - 8 : own_start, :] = nothing
        flux[at, own_end : own_end + 8, :] = nothing
        for side in range(2):
            edge_flux[side, at, 0:GUARD, :] = nothing
            edge_flux[side, at, GUARD + strip :, :] = nothing
    pack[...] = jnp.zeros(pack.shape, jnp.int32)

    local[0].wait()
    pack[0:4, 0:64] = raw_list[...]
    packed = pack[...]
    turned = pltpu.roll(packed, 64, axis=1)
    left_half = iota((1, LANES), 1) < 64
    own_list = jnp.concatenate(
        [
            jnp.where(left_half, packed[0:1], turned[1:2]),
            jnp.where(left_half, packed[2:3], turned[3:4]),
        ],
        axis=0,
    )
    lists[me] = own_list
    for copy in local[1:]:
        copy.wait()

    def unpack(start, inside, targets):
        rows = slice(start, start + 8)
        put = slice(GUARD + start, GUARD + start + 8)
        for at in range(lane_tiles):
            lanes = slice(at * LANES, (at + 1) * LANES)
            parts = [state_ext[field, rows, lanes] for field in range(4)]
            if inside is not None:
                parts = [jnp.where(inside, part, 0.0) for part in parts]
            for target, target_rows in targets:
                for field in range(4):
                    target[field, at, target_rows, :] = parts[field]
            wet = wet_ext[rows, lanes].astype(F32)
            if inside is not None:
                wet = jnp.where(inside, wet, 0.0)
            wwork[at, put, :] = wet
            hwork[at, put, :] = depth_ext[rows, lanes]

    edge_starts = (0, ext_rows - strip)
    for start in range(HALO, HALO + grid_rows, 8):
        targets = [(work, slice(GUARD + start, GUARD + start + 8))]
        for side in range(2):
            at_row = start - edge_starts[side]
            if 0 <= at_row < strip:
                targets.append((edge.at[side], slice(GUARD + at_row, GUARD + at_row + 8)))
        unpack(start, None, targets)

    first_lane = iota((8, LANES), 1) == 0
    end_lane = iota((8, LANES), 1) == LANES - 1

    def across(parts):
        up = [pltpu.roll(part, LANES - 1, axis=1) for part in parts] + [nothing]
        down = [nothing] + [pltpu.roll(part, 1, axis=1) for part in parts]
        return [
            jnp.where(end_lane, up[at + 1], up[at])
            - jnp.where(first_lane, down[at], down[at + 1])
            for at in range(lane_tiles)
        ]

    def advance(fields, flux, cross, first, last, shift, margin=0):
        for start in range(first, last, 8):
            rows = slice(start, start + 8)
            fixed = slice(start + shift, start + shift + 8)
            after = slice(start + 1, start + 9)
            before = slice(start - 1, start + 7)
            whole = first + margin <= start < last - margin
            if whole:
                slope_y = across([fields[0, at, rows, :] for at in range(lane_tiles)])
            flow = []
            for at in range(lane_tiles):
                wet = wwork[at, fixed, :]
                height = hwork[at, fixed, :]
                slope_x = fields[0, at, after, :] - fields[0, at, before, :]
                new_x = wet * (FRICTION * fields[1, at, rows, :] - PRESSURE * slope_x)
                flux[at, rows, :] = height * new_x
                if not whole:
                    continue
                new_y = wet * (FRICTION * fields[2, at, rows, :] - PRESSURE * slope_y[at])
                fields[1, at, rows, :] = new_x
                fields[2, at, rows, :] = new_y
                flow.append(height * new_y)
            if whole:
                for at, part in enumerate(across(flow)):
                    cross[at, rows, :] = part
        for start in range(last - margin - 8, first + margin - 8, -8):
            rows = slice(start, start + 8)
            fixed = slice(start + shift, start + shift + 8)
            after = slice(start + 1, start + 9)
            before = slice(start - 1, start + 7)
            for at in range(lane_tiles):
                wet = wwork[at, fixed, :]
                level = fields[0, at, rows, :]
                energy = fields[3, at, rows, :]
                spill = (flux[at, after, :] - flux[at, before, :]) + cross[at, rows, :]
                fields[0, at, rows, :] = wet * (level - DIVERGE * spill + FORCING * energy)
                fields[3, at, rows, :] = wet * (
                    (1.0 - UPWIND - DAMPING) * energy + UPWIND * fields[3, at, before, :]
                )

    def inner_step(step, carry):
        advance(work, flux, cross, own_start, own_end, 0)
        return carry

    pl.semaphore_wait(barrier, others + 2)

    halos = []
    for way, (target, source_row, target_row, source_line, target_line) in enumerate(
        (
            (below, grid_rows - HALO, 0, own_table - TABLE_PAD, 0),
            (above, 0, HALO + grid_rows, 0, TABLE_PAD + own_table),
        )
    ):
        source_rows, target_rows = pl.ds(source_row, HALO), pl.ds(target_row, HALO)
        source_lines, target_lines = pl.ds(source_line, TABLE_PAD), pl.ds(target_line, TABLE_PAD)
        pairs = [
            (state_ref.at[0, :, source_rows], state_ext.at[:, target_rows]),
            (depth_ref.at[source_rows], depth_ext.at[target_rows]),
            (wet_ref.at[source_rows], wet_ext.at[target_rows]),
        ] + [(ref.at[source_lines], ext.at[target_lines]) for ref, ext in tables]
        for i, (source, destination) in enumerate(pairs):
            copy = pltpu.make_async_remote_copy(
                src_ref=source,
                dst_ref=destination,
                send_sem=halo_send.at[way, i],
                recv_sem=halo_recv.at[way, i],
                device_id={"tile": target},
                device_id_type=MESH,
            )
            halos.append(copy)

    for i in range(7):
        for way in range(2):
            halos[way * 7 + i].start()

    def send(which, peer, source, destination):
        pltpu.make_async_remote_copy(
            src_ref=source,
            dst_ref=destination,
            send_sem=group_send.at[which],
            recv_sem=group_recv.at[which],
            device_id={"member": peer},
            device_id_type=MESH,
        ).start()

    def to_group(which, source, destination):
        def one(step, carry):
            peer = lax.rem(me + step, members)
            send(which, peer, source(peer), destination)
            return carry

        lax.fori_loop(1, members, one, 0)

    def group_done(sems, which, ref, size):
        part = ref.at[pl.ds(0, size)]
        pltpu.make_async_copy(part, part, sems.at[which]).wait()

    to_group(0, lambda peer: lists.at[me], lists.at[me])
    lax.fori_loop(0, STEPS, inner_step, 0)

    slab = 2 * lane_tiles
    edge_owners = HALO // 4

    def build(field, first, last):
        for at in range(lane_tiles):
            slab_out[
                field, pl.ds(first * slab + at, 2 * (last - first), stride=lane_tiles), :
            ] = work[field, at, own_start + 2 * first : own_start + 2 * last, :]

    def slab_of(ref, fields, owner):
        return ref.at[
            pl.ds(fields[0], len(fields)), pl.ds(pl.multiple_of(owner * slab, slab), slab)
        ]

    def slabs_done(sems, which, ref, fields):
        part = ref.at[pl.ds(fields[0], len(fields)), pl.ds(0, others * slab)]
        pltpu.make_async_copy(part, part, sems.at[which]).wait()

    def send_slabs(chunk, first, last):
        count = last - first

        def one(step, carry):
            peer = first + lax.rem(me + step, count)

            @pl.when(peer != me)
            def _():
                fields = OUTWARD[chunk]
                send(2 + chunk, peer, slab_of(slab_out, fields, peer), slab_of(slab_in, fields, me))

            return carry

        lax.fori_loop(0, count, one, 0)

    if members > 2 * edge_owners:
        for field in range(4):
            build(field, edge_owners, members - edge_owners)
        send_slabs(0, edge_owners, members - edge_owners)

    for copy in halos:
        copy.wait_recv()
    for start in range(0, HALO, 8):
        unpack(start, tile > 0, [(edge.at[0], slice(GUARD + start, GUARD + start + 8))])
    for start in range(HALO + grid_rows, ext_rows, 8):
        at_row = start - edge_starts[1]
        unpack(
            start,
            tile < tiles - 1,
            [(edge.at[1], slice(GUARD + at_row, GUARD + at_row + 8))],
        )

    def edge_step(margin):
        for side in range(2):
            advance(
                edge.at[side],
                edge_flux.at[side],
                edge_cross.at[side],
                GUARD,
                GUARD + strip,
                edge_starts[side],
                margin,
            )

    def outer_step(step, carry):
        edge_step(0)
        return carry

    lax.fori_loop(0, STEPS - 1, outer_step, 0)
    edge_step(8)

    def from_edges(field):
        for side in range(2):
            for start in (GUARD + 8, GUARD + 16):
                for at in range(lane_tiles):
                    put = start + edge_starts[side]
                    work[field, at, put : put + 8, :] = edge[side, field, at, start : start + 8, :]

    from_edges(0)

    first_line = TABLE_PAD - OBS_HALO // 2
    last_line = TABLE_PAD + own_table + OBS_HALO // 2
    offset = (cell_ext[...] & (SPACING - 1)).astype(BF16)
    place = iota((1, LANES), 1) & (SPACING - 1)
    chosen = [[], [], []]
    gathers = []
    for parity in range(2):
        for at in range(lane_tiles):
            owner = iota((LANES, LANES), 0) // SPACING + (parity * 64 + at * 16)
            gathers.append((owner == iota((LANES, LANES), 1)).astype(BF16))
            owner_t = iota((LANES, LANES), 1) // SPACING + (parity * 64 + at * 16)
            scatter = (owner_t == iota((LANES, LANES), 0)).astype(BF16)
            wanted = dot(offset, scatter).astype(jnp.int32) == place
            level = work[0, at, pl.ds(GUARD + parity, table_rows, stride=2), :]
            level = jnp.where(wanted, level, 0.0)
            for part, piece in zip(chosen, split3(level)):
                part.append(piece)
    gather = jnp.concatenate(gathers, axis=0)
    pieces = [dot(jnp.concatenate(part, axis=1), gather) for part in chosen]
    table[...] = ((pieces[2] + pieces[1]) + pieces[0]) * gain_ext[...]

    group_done(group_recv, 0, lists, others)
    base = obs_tile - TABLE_PAD * LANES
    for start in range(0, members, 4):
        slots = jnp.concatenate([lists[start + i] for i in range(4)], axis=0) - base
        found = lookup(
            table, first_line, last_line, slots // LANES, slots & (LANES - 1)
        )
        for i in range(4):
            pick_out[start + i] = found[2 * i : 2 * i + 2, :]
    to_group(1, lambda peer: pick_out.at[peer], pick_in.at[me])
    pick_in[me] = pick_out[me]

    for field in range(1, 4):
        from_edges(field)
    for field in range(4):
        build(field, 0, edge_owners)
        build(field, members - edge_owners, members)
    send_slabs(0, 0, edge_owners)
    send_slabs(0, members - edge_owners, members)
    send_slabs(1, 0, members)
    own_slab = pl.ds(pl.multiple_of(me * slab, slab), slab)
    for field in range(4):
        slab_in[field, own_slab, :] = slab_out[field, own_slab, :]

    names = jnp.concatenate([own_list] * 4, axis=0)
    slots = names - base
    high, low = slots // LANES, slots & (LANES - 1)
    value = lookup(value_ext, first_line, last_line, high, low)
    error = lookup(error_ext, first_line, last_line, high, low)
    value, error = value[0:2], error[0:2]
    row_index = me * 2 + iota((2, LANES), 0)
    centre = obs_tile + row_index * 64
    dist = (own_list - centre).astype(F32) / radius
    counts = raw_count[...]
    slot = iota((1, LANES), 1) & 63
    limit = jnp.concatenate(
        [
            jnp.where(
                left_half, counts[0:1, 2 * i : 2 * i + 1], counts[0:1, 2 * i + 1 : 2 * i + 2]
            )
            for i in range(2)
        ],
        axis=0,
    )
    live = slot < limit
    precision = jnp.where(live, 1.0 / ((1.0 + 4.0 * dist * dist) * error), 0.0)

    size = 4 * members
    patch_of_line = iota((size, 2 * LANES), 0) // members
    patch_of_slot = iota((size, 2 * LANES), 1) // 64
    line, column = iota((size, size), 0) // members, iota((size, size), 1) // members
    same = line == column
    diagonal = iota((members, size), 0) == iota((members, size), 1) % members
    eye = jnp.where(diagonal, 1.0, 0.0)
    ones = jnp.where(same, 1.0, 0.0).astype(BF16)
    patch_ones = (iota((2 * LANES, size), 0) // 64 == iota((2 * LANES, size), 1) // members)
    patch_ones = jnp.where(patch_ones, 1.0, 0.0).astype(BF16)

    def blocks(packed):
        return jnp.where(same, jnp.concatenate([packed] * 4, axis=0), 0.0)

    group_done(group_recv, 1, pick_in, others)
    picked = jnp.concatenate([pick_in[:, i, :] for i in range(2)], axis=1)
    mean_eq = jnp.sum(picked, axis=0, keepdims=True) * (1.0 / members)
    spread = picked - mean_eq
    precision = jnp.concatenate([precision[0:1], precision[1:2]], axis=1)
    value = jnp.concatenate([value[0:1], value[1:2]], axis=1)
    weighted = spread * precision
    by_patch = jnp.where(
        patch_of_line == patch_of_slot, jnp.concatenate([spread] * 4, axis=0), 0.0
    )
    innovation = jnp.broadcast_to(precision * (value - mean_eq), weighted.shape)
    sums = lax.dot_general(
        jnp.concatenate([weighted, innovation], axis=0),
        by_patch,
        (((1,), (1,)), ((), ())),
        precision=HIGH,
        preferred_element_type=F32,
    )
    gram, proj = sums[:members], sums[members:]
    squares = exact_dot(weighted * spread, patch_ones)
    trace = jnp.sum(squares, axis=0, keepdims=True) + (members - 1.0) * members

    amat = gram + (members - 1.0) * eye

    def times(left, right):
        return dot6(left, blocks(right))

    def two_steps(square):
        second = times(square, square)
        third, fourth = times(second, square), times(second, second)
        after = 2.25 * square - 1.5 * second + 0.25 * third
        both = 2.25 * second - 1.5 * third + 0.25 * fourth
        return second, 2.25 * eye - 0.75 * (after + square) + 0.25 * both

    def three_steps(step, carry):
        square, inverse = carry
        second, factor = two_steps(square)
        once, twice = times(square, factor), times(second, factor)
        squared = times(factor, factor)
        product = 1.5 * factor - 0.5 * times(once, squared)
        moved = 1.5 * once - 0.5 * times(twice, squared)
        return times(moved, product), times(product, inverse)

    square, inverse = lax.fori_loop(0, (NS_ITERS - 2) // 3, three_steps, (amat / trace, eye))
    scale = (members - 1.0) ** 0.5 / jnp.sqrt(trace)
    early = times(proj, inverse)
    total = exact_dot(inverse, ones)
    _, factor = two_steps(square)
    early = times(early, factor)
    inverse = times(factor, inverse)
    total = times(factor, total)
    wbar = times(early, inverse) - times(early, total) * (1.0 / members)
    mix = scale * (inverse - total * (1.0 / members)) + wbar / trace + 1.0 / members
    mix = blocks(mix)
    mix_high, mix_low = split(mix)
    mix_both = jnp.concatenate([mix_high, mix_low], axis=0)

    for chunk, fields in enumerate(BACK):
        for field in fields:
            for coming, arriving in enumerate(OUTWARD):
                if field == arriving[0]:
                    slabs_done(group_recv, 2 + coming, slab_in, arriving)
            lines = [
                [
                    slab_in[field, pl.ds(row * lane_tiles + at, members, stride=slab), :]
                    for at in range(lane_tiles)
                ]
                for row in range(2)
            ]
            inputs = jnp.concatenate(
                [
                    jnp.concatenate(lines[row][2 * side : 2 * side + 2], axis=1)
                    for row in range(2)
                    for side in range(2)
                ],
                axis=0,
            )
            high, low = split(inputs)
            both = dot(mix_both, high)
            mixed = (both[size:] + dot(mix_high, low)) + both[:size]
            for row in range(2):
                for at in range(lane_tiles):
                    patch = row * 2 + at // 2
                    mix_out[
                        field, pl.ds(row * lane_tiles + at, members, stride=slab), :
                    ] = mixed[
                        patch * members : (patch + 1) * members,
                        (at % 2) * LANES : (at % 2 + 1) * LANES,
                    ]
        to_group(
            4 + chunk,
            lambda peer: slab_of(mix_out, fields, peer),
            slab_of(back_in, fields, me),
        )
        for field in fields:
            back_in[field, own_slab, :] = mix_out[field, own_slab, :]
    for chunk, fields in enumerate(BACK):
        slabs_done(group_recv, 4 + chunk, back_in, fields)
        for field in fields:
            for at in range(lane_tiles):
                out_ref[0, field, :, at * LANES : (at + 1) * LANES] = back_in[
                    field, pl.ds(at, grid_rows, stride=lane_tiles), :
                ]

    for copy in halos:
        copy.wait_send()
    group_done(group_send, 0, lists, others)
    group_done(group_send, 1, pick_out, others)
    for chunk, fields in enumerate(OUTWARD):
        slabs_done(group_send, 2 + chunk, slab_out, fields)
    for chunk, fields in enumerate(BACK):
        slabs_done(group_send, 4 + chunk, mix_out, fields)


def body(
    realization_array,
    water_depth,
    wet_mask,
    obs_cell,
    obs_value,
    obs_error,
    celer_gain,
    obs_list,
    obs_count,
):
    members = lax.axis_size("member")
    tiles = lax.axis_size("tile")
    grid_rows, width = water_depth.shape
    ext_rows = grid_rows + 2 * HALO
    lane_tiles = width // LANES
    own_table = obs_cell.shape[0] // LANES
    table_rows = own_table + 2 * TABLE_PAD
    slab_rows = members * 2 * lane_tiles
    strip = 2 * HALO + 2 * GUARD
    deep = ext_rows + 2 * GUARD
    as_lines = lambda array: array.reshape(own_table, LANES)
    far = pl.BlockSpec(memory_space=pltpu.HBM)
    near = pl.BlockSpec(memory_space=pltpu.VMEM)
    return pl.pallas_call(
        functools.partial(kernel, members, tiles, grid_rows),
        out_shape=jax.ShapeDtypeStruct(realization_array.shape, F32),
        in_specs=[far] * 9,
        out_specs=near,
        scratch_shapes=[
            pltpu.VMEM((4, ext_rows, width), F32),
            pltpu.VMEM((ext_rows, width), F32),
            pltpu.VMEM((ext_rows, width), jnp.int32),
            pltpu.VMEM((table_rows, LANES), jnp.int32),
            pltpu.VMEM((table_rows, LANES), F32),
            pltpu.VMEM((table_rows, LANES), F32),
            pltpu.VMEM((table_rows, LANES), F32),
            pltpu.VMEM((4, lane_tiles, deep, LANES), F32),
            pltpu.VMEM((2, 4, lane_tiles, strip, LANES), F32),
            pltpu.VMEM((lane_tiles, deep, LANES), F32),
            pltpu.VMEM((lane_tiles, deep, LANES), F32),
            pltpu.VMEM((lane_tiles, deep, LANES), F32),
            pltpu.VMEM((lane_tiles, deep, LANES), F32),
            pltpu.VMEM((2, lane_tiles, strip, LANES), F32),
            pltpu.VMEM((2, lane_tiles, strip, LANES), F32),
            pltpu.VMEM(obs_list.shape[1:], jnp.int32),
            pltpu.VMEM(obs_count.shape, jnp.int32),
            pltpu.VMEM((8, LANES), jnp.int32),
            pltpu.VMEM((members, 2, LANES), jnp.int32),
            pltpu.VMEM((table_rows, LANES), F32),
            pltpu.VMEM((members, 2, LANES), F32),
            pltpu.VMEM((members, 2, LANES), F32),
            pltpu.VMEM((4, slab_rows, LANES), F32),
            pltpu.VMEM((4, slab_rows, LANES), F32),
            pltpu.VMEM((4, slab_rows, LANES), F32),
            pltpu.VMEM((4, slab_rows, LANES), F32),
            pltpu.SemaphoreType.DMA((9,)),
            pltpu.SemaphoreType.DMA((2, 7)),
            pltpu.SemaphoreType.DMA((2, 7)),
            pltpu.SemaphoreType.DMA((4 + len(BACK),)),
            pltpu.SemaphoreType.DMA((4 + len(BACK),)),
        ],
        compiler_params=pltpu.CompilerParams(
            collective_id=0, has_side_effects=True, vmem_limit_bytes=32 * 1024 * 1024
        ),
    )(
        *[
            pltpu.with_memory_space_constraint(array, pltpu.HBM)
            for array in (
                realization_array,
                water_depth,
                wet_mask,
                as_lines(obs_cell),
                as_lines(celer_gain),
                as_lines(obs_value),
                as_lines(obs_error),
                obs_list,
                obs_count,
            )
        ]
    )


def solution(mesh):
    return jax.shard_map(
        body,
        mesh=mesh,
        in_specs=(
            P("member", None, "tile", None),
            P("tile", None),
            P("tile", None),
            P("tile"),
            P("tile"),
            P("tile"),
            P("tile"),
            P("tile", "member", None),
            P("tile", "member"),
        ),
        out_specs=P("member", None, "tile", None),
        check_vma=False,
    )
```
